32 devices in a mesh: tm: 8 (over z, y), region: 4 (over x, core).
Axes of the slice: x: 2, y: 2, z: 4, core: 2. Of those that a mesh axis runs over, the one named last changes fastest.
Arguments:
- covariates: bfloat16 [8, 1024, 256], P('region', 'tm'), may hold values from -4 to 4
- observed: float32 [8, 1024, 256], P('region', 'tm'), may hold values from -40 to 40
- input_weight: bfloat16 [256, 256], replicated, may hold values from -0.375 to 0.375
- filter_weight: bfloat16 [3, 512, 512], replicated, may hold values from -0.25 to 0.25
- mixing_weight: bfloat16 [3, 256, 256], replicated, may hold values from -0.375 to 0.375
- output_weight: bfloat16 [256, 4096], replicated, may hold values from -0.375 to 0.375
Outputs:
- covariate_grad: bfloat16 [8, 1024, 256], P('region', 'tm')
- input_grad: bfloat16 [256, 256], P('tm')
- filter_grad: bfloat16 [3, 512, 512], P(None, 'tm')
- mixing_grad: bfloat16 [3, 256, 256], P(None, 'tm')
- output_grad: bfloat16 [256, 4096], P('tm')
The draws below stay inside these ranges and needn't reach their ends.
All inputs are finite; a program needn't handle non-finite values.
Results may differ from the reference program's by a relative error of at most 0.022.
Values may be sent and summed in bfloat16 or wider, within the bound.
A program may use at most 64 MiB of HBM per device.

```python
import math
import jax
import jax.numpy as jnp
from jax import lax

NODES = 256
WIDTH = 256
SCENARIOS = 16
LAYERS = 3
SEQS = 8
STEPS = 1024


def draw_observed(key, part):
    key_base, key_nodes = jax.random.split(key, 2)
    position = jnp.arange(STEPS, dtype=jnp.float32) / (STEPS - 1)
    ramp = 0.05 * jnp.exp(math.log(60.0) * position)
    node_scale = jnp.exp(jax.random.uniform(key_nodes, (SEQS, 1, NODES), jnp.float32, math.log(0.3), math.log(3.0)))
    base = jnp.clip(jax.random.normal(key_base, (SEQS, STEPS, NODES), jnp.float32), -4.0, 4.0)
    return (base * ramp[None, :, None] * node_scale).astype(jnp.float32)


def draw_output_weight(key, part):
    key_entries, key_order, key_jitter = jax.random.split(jax.random.fold_in(key, 7), 3)
    order = jax.random.permutation(key_order, SCENARIOS).astype(jnp.float32)
    jitter = jax.random.uniform(key_jitter, (SCENARIOS,), jnp.float32, 0.0, 1.0)
    factor = jnp.exp(math.log(0.1) * (order + jitter) / SCENARIOS)
    column_factor = jnp.repeat(factor, NODES)
    entries = jax.random.normal(key_entries, (WIDTH, SCENARIOS * NODES), jnp.float32)
    values = entries * WIDTH ** (-0.5) * column_factor[None, :]
    return jnp.clip(values, -0.375, 0.375).astype(jnp.bfloat16)


def levels(stream_key, dims, pieces, least, largest):
    def one(axis_at, shards_of):
        draws = jax.random.uniform(jax.random.fold_in(jax.random.fold_in(stream_key, 6), axis_at), (shards_of,), jnp.float32, least / len(pieces), largest / len(pieces))
        return jnp.repeat(jnp.exp(draws), dims[axis_at] // shards_of).reshape((-1,) + (1,) * (len(dims) - axis_at - 1))

    factor_of = one(*pieces[0])
    for cut in pieces[1:]:
        factor_of = factor_of * one(*cut)
    return factor_of


def gaussian(own_key, dims, deviation, limit, cuts=(), held_as=jnp.bfloat16):
    loudness = levels(own_key, dims, cuts, -0.22, 0.18) if cuts else 1.0
    result = jax.random.normal(own_key, dims, jnp.float32) * deviation * loudness
    return jnp.minimum(jnp.maximum(result, -limit), limit).astype(held_as)


def setup_inputs(seed: int = 0) -> dict:
    streams_of = jax.random.split(jax.random.key(seed), 7)
    covariates = gaussian(streams_of[0], (SEQS, STEPS, NODES), 1.0, 4.0, ((0, 4), (1, 8)))
    observed = draw_observed(jax.random.fold_in(streams_of[6], 71), 0)
    input_weight = gaussian(streams_of[2], (NODES, WIDTH), NODES ** -0.5, 0.375)
    filter_weight = gaussian(streams_of[3], (LAYERS, 2 * WIDTH, 2 * WIDTH), (2 * WIDTH) ** -0.5, 0.25)
    mixing_weight = gaussian(streams_of[4], (LAYERS, WIDTH, WIDTH), WIDTH ** -0.5, 0.375)
    output_weight = draw_output_weight(jax.random.fold_in(streams_of[6], 71), 0)
    return {"covariates": covariates, "observed": observed, "input_weight": input_weight, "filter_weight": filter_weight, "mixing_weight": mixing_weight, "output_weight": output_weight}


epsilon = 1e-05

def energy(predicted, observed, scenarios):
    node_count = observed.shape[-1]
    scenario_vals = predicted.reshape(predicted.shape[:-1] + (scenarios, node_count))
    gram_matrix = jnp.einsum('...sn,...rn->...sr', scenario_vals, scenario_vals, precision=lax.Precision.HIGHEST)
    against = jnp.einsum('...sn,...n->...s', scenario_vals, observed, precision=lax.Precision.HIGHEST)
    own_sq = jnp.diagonal(gram_matrix, axis1=-2, axis2=-1)
    target = lax.optimization_barrier(jnp.sum(observed * observed, axis=-1))
    to_target = jnp.sqrt((own_sq - 2.0 * against + target[..., None]) / node_count + epsilon)
    off_diag = 1.0 - jnp.eye(scenarios, dtype=jnp.float32)
    pair_sq = (own_sq[..., :, None] + own_sq[..., None, :] - 2.0 * gram_matrix) / node_count
    between = jnp.sqrt(pair_sq * off_diag + epsilon) * off_diag
    return lax.optimization_barrier(jnp.mean(to_target, axis=-1)) - lax.optimization_barrier(jnp.sum(between, axis=(-2, -1))) / (2.0 * scenarios * (scenarios - 1))

def network(weights, cov_seq):
    w_input, w_filter, w_mixing, w_output = weights
    length = cov_seq.shape[0]
    hidden = jnp.dot(cov_seq, w_input, preferred_element_type=jnp.float32).astype(jnp.bfloat16)
    channels = hidden.shape[-1]
    for layer_no in range(w_filter.shape[0]):
        dilation = 2 ** layer_no
        delayed = jnp.pad(hidden, ((dilation, 0), (0, 0)))[:length]
        joined = jnp.concatenate([delayed, hidden], axis=-1)
        preact = jnp.dot(joined, w_filter[layer_no], preferred_element_type=jnp.float32)
        gated = (jnp.tanh(preact[:, :channels]) * jax.nn.sigmoid(preact[:, channels:])).astype(jnp.bfloat16)
        hidden = (hidden.astype(jnp.float32) + jnp.dot(gated, w_mixing[layer_no], preferred_element_type=jnp.float32)).astype(jnp.bfloat16)
    return jnp.dot(hidden, w_output, preferred_element_type=jnp.float32)

def reference(covariates, observed, input_weight, filter_weight, mixing_weight, output_weight):
    scale = jnp.sqrt(lax.optimization_barrier(jnp.mean(observed * observed, axis=(1, 2))) + epsilon)
    weights = (input_weight.astype(jnp.float32), filter_weight.astype(jnp.float32), mixing_weight.astype(jnp.float32), output_weight.astype(jnp.float32))

    def per_sequence(running, inputs_seq):
        cov_seq, obs_seq, seq_scale = inputs_seq

        def scoring(weight_set, cov_part):
            return jnp.sum(energy(network(weight_set, cov_part), obs_seq, SCENARIOS)) / seq_scale
        _, pull_back = jax.vjp(scoring, weights, cov_seq)
        grads_w, grad_cov = pull_back(jnp.ones((), jnp.float32))
        running = tuple((first + second for first, second in zip(running, grads_w)))
        return (running, grad_cov)
    zeros_init = tuple((jnp.zeros_like(weight_one) for weight_one in weights))
    totals, covariate_grad = lax.scan(per_sequence, zeros_init, (covariates, observed, scale))
    return (covariate_grad, totals[0].astype(jnp.bfloat16), totals[1].astype(jnp.bfloat16), totals[2].astype(jnp.bfloat16), totals[3].astype(jnp.bfloat16))
```

```python
import functools

import jax
import jax.numpy as jnp
from jax import lax
from jax.experimental import pallas as pl
from jax.experimental.pallas import tpu as pltpu
from jax.sharding import PartitionSpec as P

MESH = pl.DeviceIdType.MESH
epsilon = 1e-05
HALO = 8
F32 = jnp.float32
BF16 = jnp.bfloat16


def dot(a, b, ca=1, cb=0, precision=None):
    return lax.dot_general(
        a, b, (((ca,), (cb,)), ((), ())), precision=precision, preferred_element_type=F32
    )


def edges_kernel(
    nt, cov, obs, prev_cov, next_cov, next_obs, total,
    got_prev, got_next, got_obs, sums, send_sem, recv_sem,
):
    me = lax.axis_index("tm")
    rows = cov.shape[1]

    def at(offset):
        return {"tm": lax.rem(me + offset, nt)}

    barrier = pltpu.get_barrier_semaphore()
    for offset in range(1, nt):
        pl.semaphore_signal(barrier, inc=1, device_id=at(offset), device_id_type=MESH)
    sq = obs[...] * obs[...]
    seqs, _, nodes = obs.shape
    sq = jnp.sum(sq.reshape(seqs, rows // 8, 8, nodes), axis=1)
    own = sq[:, :, :128]
    for part in range(1, nodes // 128):
        own = own + sq[:, :, part * 128 : (part + 1) * 128]
    sums[0] = own
    pl.semaphore_wait(barrier, nt - 1)
    copies = []

    def send(src, dst, offset):
        slot = len(copies)
        copy = pltpu.make_async_remote_copy(
            src_ref=src, dst_ref=dst, send_sem=send_sem.at[slot], recv_sem=recv_sem.at[slot],
            device_id=at(offset), device_id_type=MESH,
        )
        copy.start()
        copies.append(copy)

    send(cov.at[:, pl.ds(rows - 16, 16), :], got_prev, 1)
    send(cov.at[:, pl.ds(0, 16), :], got_next, nt - 1)
    send(obs.at[:, pl.ds(0, HALO), :], got_obs, nt - 1)
    for offset in range(1, nt):
        send(sums.at[0], sums.at[offset], offset)
    for copy in copies:
        copy.wait()
    prev_cov[...] = got_prev[...]
    next_cov[...] = got_next[...]
    next_obs[...] = got_obs[...]
    total[...] = jnp.sum(sums[...], axis=0)


def exchange_edges(nt, cov, obs):
    seqs, rows, nodes = cov.shape
    vmem = pl.BlockSpec(memory_space=pltpu.VMEM)
    edge = jax.ShapeDtypeStruct((seqs, 16, nodes), BF16)
    copies = nt + 2
    return pl.pallas_call(
        functools.partial(edges_kernel, nt),
        out_shape=(
            edge,
            edge,
            jax.ShapeDtypeStruct((seqs, HALO, nodes), F32),
            jax.ShapeDtypeStruct((seqs, 8, 128), F32),
        ),
        in_specs=[vmem] * 2,
        out_specs=(vmem,) * 4,
        scratch_shapes=[
            pltpu.VMEM((seqs, 16, nodes), BF16),
            pltpu.VMEM((seqs, 16, nodes), BF16),
            pltpu.VMEM((seqs, HALO, nodes), F32),
            pltpu.VMEM((nt, seqs, 8, 128), F32),
            pltpu.SemaphoreType.DMA((copies,)),
            pltpu.SemaphoreType.DMA((copies,)),
        ],
        compiler_params=pltpu.CompilerParams(collective_id=0, has_side_effects=True),
        name="edges",
    )(cov, obs)


def network_kernel(
    nt, packed,
    cov, obs, prev_cov, next_cov, next_obs, total, w_input, w_filter, w_mixing, w_output,
    cov_grad, *rest,
):
    if packed:
        grads, scen, scored = rest
    else:
        g_input, g_filter, g_mixing, g_output, scen, scored = rest
    me = lax.axis_index("tm")
    seqs, rows, nodes = cov.shape
    layers = w_filter.shape[0]
    channels = w_mixing.shape[1]
    scenarios = w_output.shape[1] // nodes
    span = rows + 2 * HALO
    kept = rows + HALO
    unit = channels // nt
    not_first = (me > 0).astype(F32)
    not_last = (me < nt - 1).astype(F32)

    def own_rows(x):
        return jnp.concatenate([x[b * span + HALO : b * span + HALO + rows] for b in range(seqs)], axis=0)

    def put(first_row, height, value):
        grads[:, first_row : first_row + height, :] = value.reshape(nt, height, nodes).astype(BF16)

    cov_own = cov[...]
    spans = []
    for b in range(seqs):
        spans.append(prev_cov[b].astype(F32)[16 - HALO :] * not_first)
        spans.append(cov_own[b].astype(F32))
        spans.append(next_cov[b].astype(F32)[:HALO])
    hidden = dot(jnp.concatenate(spans, axis=0).astype(BF16), w_input[...]).astype(BF16).astype(F32)
    stored = []
    for l in range(layers):
        delayed = pltpu.roll(hidden, 2**l, 0)
        joined = jnp.concatenate([delayed, hidden], axis=1).astype(BF16)
        preact = dot(joined, w_filter[l])
        act = jnp.tanh(preact[:, :channels])
        gate = 0.5 * jnp.tanh(0.5 * preact[:, channels:]) + 0.5
        gated = (act * gate).astype(BF16)
        stored.append((delayed, hidden, act, gate))
        hidden = (hidden + dot(gated, w_mixing[l])).astype(BF16).astype(F32)

    last = jnp.concatenate([hidden[b * span + HALO : (b + 1) * span] for b in range(seqs)], axis=0)
    last = last.astype(BF16)
    for s in range(scenarios):
        pred = dot(last, w_output[:, s * nodes : (s + 1) * nodes])
        for half in range(nodes // 128):
            scen[half, pl.ds(s, seqs * kept, stride=scenarios), :] = pred[:, half * 128 : (half + 1) * 128]
    for b in range(seqs):
        scored[b * kept : b * kept + rows] = obs[b]
        scored[b * kept + rows : (b + 1) * kept] = next_obs[b]

    block = 16 * scenarios
    row_no = lax.broadcasted_iota(jnp.int32, (block, block), 0)
    col_no = lax.broadcasted_iota(jnp.int32, (block, block), 1)
    same_step = (row_no // scenarios) == (col_no // scenarios)
    diagonal = row_no == col_no
    pairs = jnp.where(same_step & ~diagonal, 1.0 / (scenarios * (scenarios - 1) * nodes), 0.0)
    halves = nodes // 128

    def score(g, carry):
        at = pl.ds(pl.multiple_of(g * block, block), block)
        y = jnp.concatenate([scen[h, at, :] for h in range(halves)], axis=1)
        o = scored[pl.ds(pl.multiple_of(g * 16, 16), 16), :]
        o = jnp.broadcast_to(o[:, None, :], (16, scenarios, nodes)).reshape(block, nodes)
        gram = dot(y, y, 1, 1, lax.Precision.HIGHEST)
        own = jnp.where(diagonal, gram, 0.0)
        own_sq = jnp.sum(own, axis=1, keepdims=True) + jnp.sum(own, axis=0, keepdims=True)
        pair_sq = jnp.maximum(own_sq - 2.0 * gram, 0.0) * (1.0 / nodes)
        coef = pairs * lax.rsqrt(pair_sq + epsilon)
        mixed = dot(coef, y, 1, 0, lax.Precision.HIGHEST)
        diff = y - o
        target = lax.rsqrt(jnp.sum(diff * diff, axis=1, keepdims=True) * (1.0 / nodes) + epsilon)
        target = target * (1.0 / (scenarios * nodes))
        grad = mixed - jnp.sum(coef, axis=1, keepdims=True) * y + target * diff
        for h in range(halves):
            scen[h, at, :] = grad[:, h * 128 : (h + 1) * 128]
        return carry

    lax.fori_loop(0, seqs * kept // 16, score, 0)

    length = rows * nt
    step_no = lax.broadcasted_iota(jnp.int32, (kept, 1), 0)
    valid = jnp.where(step_no < rows, 1.0, not_last)
    factor = []
    for b in range(seqs):
        sq = jnp.sum(jnp.sum(total[b], axis=1, keepdims=True), axis=0, keepdims=True)
        factor.append(valid * lax.rsqrt(sq / (length * nodes) + epsilon))
    factor = jnp.concatenate(factor, axis=0)

    def kept_own(x):
        return jnp.concatenate([x[b * kept : b * kept + rows] for b in range(seqs)], axis=0)

    last_own = own_rows(hidden).T.astype(BF16)
    grad_last = jnp.zeros((seqs * kept, channels), F32)
    for s in range(scenarios):
        g = jnp.concatenate(
            [scen[h, pl.ds(s, seqs * kept, stride=scenarios), :] for h in range(halves)], axis=1
        )
        g = g * factor
        grad_last = grad_last + dot(g.astype(BF16), w_output[:, s * nodes : (s + 1) * nodes], 1, 1)
        part = dot(last_own, kept_own(g).astype(BF16))
        if packed:
            put(s * unit, unit, part)
        else:
            g_output[:, s * nodes : (s + 1) * nodes] = part.astype(BF16)
    grad_last = grad_last.astype(BF16).astype(F32)
    pieces = []
    for b in range(seqs):
        pieces.append(jnp.zeros((HALO, channels), F32))
        pieces.append(grad_last[b * kept : (b + 1) * kept])
    grad = jnp.concatenate(pieces, axis=0)

    first = scenarios * unit
    for l in reversed(range(layers)):
        delayed, held, act, gate = stored[l]
        grad16 = grad.astype(BF16)
        gated_t = own_rows(act * gate).T.astype(BF16)
        part = dot(gated_t, own_rows(grad).astype(BF16))
        if packed:
            put(first + layers * 4 * unit + l * unit, unit, part)
        else:
            g_mixing[l] = part.astype(BF16)
        gated_cot = dot(grad16, w_mixing[l], 1, 1).astype(BF16).astype(F32)
        pre = jnp.concatenate(
            [gated_cot * gate * (1.0 - act * act), gated_cot * act * gate * (1.0 - gate)], axis=1
        )
        own_pre = own_rows(pre).astype(BF16)
        for tap, source in enumerate((delayed, held)):
            part = dot(own_rows(source).T.astype(BF16), own_pre)
            if packed:
                owners = nt // 2
                height = 2 * unit
                for half in range(2):
                    piece = part[:, half * nodes : (half + 1) * nodes].reshape(owners, height, nodes)
                    at = first + (l * 2 + half) * height
                    grads[tap * owners : (tap + 1) * owners, at : at + height, :] = piece.astype(BF16)
            else:
                g_filter[l, tap * channels : (tap + 1) * channels, :] = part.astype(BF16)
        both = dot(pre.astype(BF16), w_filter[l], 1, 1).astype(BF16).astype(F32)
        past = pltpu.roll(both[:, :channels], seqs * span - 2**l, 0)
        grad = (grad + both[:, channels:] + past).astype(BF16).astype(F32)

    own = own_rows(grad).astype(BF16)
    cov_flat = jnp.concatenate([cov_own[b] for b in range(seqs)], axis=0)
    part = dot(cov_flat.astype(F32).T.astype(BF16), own)
    if packed:
        put(first + layers * 5 * unit, unit, part)
    else:
        g_input[...] = part.astype(BF16)
    result = dot(own, w_input[...], 1, 1).astype(BF16)
    for b in range(seqs):
        cov_grad[b] = result[b * rows : (b + 1) * rows]


def run_network(nt, packed, cov, obs, edges, weights):
    seqs, rows, nodes = cov.shape
    w_input, w_filter, w_mixing, w_output = weights
    scenarios = w_output.shape[1] // nodes
    vmem = pl.BlockSpec(memory_space=pltpu.VMEM)
    if packed:
        width = sum(w.size for w in weights) // nt // nodes
        grads = (jax.ShapeDtypeStruct((nt, width, nodes), BF16),)
    else:
        grads = tuple(jax.ShapeDtypeStruct(w.shape, BF16) for w in weights)
    steps = seqs * (rows + HALO)
    return pl.pallas_call(
        functools.partial(network_kernel, nt, packed),
        out_shape=(jax.ShapeDtypeStruct(cov.shape, BF16),) + grads,
        in_specs=[vmem] * 10,
        out_specs=(vmem,) * (1 + len(grads)),
        scratch_shapes=[
            pltpu.VMEM((nodes // 128, steps * scenarios, 128), F32),
            pltpu.VMEM((steps, nodes), F32),
        ],
        compiler_params=pltpu.CompilerParams(vmem_limit_bytes=56 * 2**20),
        name="network",
    )(cov, obs, *edges, *weights)


def plan(nt, nr, rows):
    bits = lambda n: n.bit_length() - 1
    tm_dims = [("tm", 2**i) for i in reversed(range(bits(nt)))]
    region_dims = [("region", 2**i) for i in reversed(range(bits(nr)))]
    near = region_dims[-1:]
    x, ys = region_dims[:-1], list(reversed(tm_dims))
    y, z = ys[:1], ys[1:]
    orders = [near + x + y + z, near + y + z[:1] + x + z[1:], near + z[:1] + x + y + z[1:]]
    units = rows // 16
    count = min(len(orders), units)
    cuts = [16 * (units * i // count) for i in range(count + 1)]
    parts = [(cuts[i], cuts[i + 1] - cuts[i], orders[i]) for i in range(count)]
    return tm_dims + region_dims, tm_dims, region_dims, parts


def reduce_kernel(nt, nr, rows, packed, shapes, grads, *refs):
    dims, tm_dims, region_dims, parts = plan(nt, nr, rows)
    n_out = len(shapes)
    outs, refs = refs[:n_out], list(refs[n_out:])
    send_sem, recv_sem = refs[-2:]
    whole = refs[-3]
    where = {"tm": lax.axis_index("tm"), "region": lax.axis_index("region")}

    def bit(dim):
        axis, weight = dim
        return lax.rem(lax.div(where[axis], weight), 2)

    def across(dim):
        axis, weight = dim
        return {axis: where[axis] + weight * (1 - 2 * bit(dim))}

    barrier = pltpu.get_barrier_semaphore()
    for dim in dims:
        pl.semaphore_signal(barrier, inc=1, device_id=across(dim), device_id_type=MESH)
    pl.semaphore_wait(barrier, len(dims))

    slot = 0
    state = []
    for i, (start, height, order) in enumerate(parts):
        buffers = refs[i * len(dims) : (i + 1) * len(dims)]
        state.append([grads, list(dims), buffers])

    def start_copy(src, dst, dim):
        nonlocal slot
        copy = pltpu.make_async_remote_copy(
            src_ref=src, dst_ref=dst, send_sem=send_sem.at[slot], recv_sem=recv_sem.at[slot],
            device_id=across(dim), device_id_type=MESH,
        )
        slot += 1
        copy.start()
        return copy

    def half(i, dim, side):
        left = state[i][1]
        rows_at = pl.ds(parts[i][0], parts[i][1]) if state[i][0] is grads else slice(None)
        return tuple(side if d == dim else slice(None) for d in left) + (rows_at, slice(None))

    def send_half(i, phase):
        dim = parts[i][2][phase]
        return start_copy(state[i][0].at[half(i, dim, 1 - bit(dim))], state[i][2][phase], dim)

    def gather_at(dim):
        place = region_dims.index(dim)
        return tuple(bit(d) if n <= place else slice(None) for n, d in enumerate(region_dims))

    def send_whole(i, n):
        dim = list(region_dims)[n]
        index = tuple(slice(None) if m < n else bit(d) for m, d in enumerate(region_dims))
        index = index + (pl.ds(parts[i][0], parts[i][1]), slice(None))
        return start_copy(whole.at[index], whole.at[index], dim)

    flying = [send_half(i, 0) for i in range(len(parts))]
    done = []
    for phase in range(len(dims)):
        for i in range(len(parts)):
            dim = parts[i][2][phase]
            flying[i].wait_recv()
            done.append(flying[i])
            source, left, buffers = state[i]
            into = buffers[phase]
            mine = source[half(i, dim, bit(dim))]
            into[...] = (into[...].astype(F32) + mine.astype(F32)).astype(BF16)
            state[i][0] = into
            state[i][1] = [d for d in left if d != dim]
            if phase + 1 < len(dims):
                flying[i] = send_half(i, phase + 1)
            else:
                index = tuple(bit(d) for d in region_dims)
                whole[index + (pl.ds(parts[i][0], parts[i][1]), slice(None))] = into[...]
                flying[i] = send_whole(i, 0)
    for n in range(len(region_dims)):
        for i in range(len(parts)):
            flying[i].wait_recv()
            done.append(flying[i])
            if n + 1 < len(region_dims):
                flying[i] = send_whole(i, n + 1)
    for copy in done:
        copy.wait_send()

    if not packed:
        outs[0][...] = whole[...]
        return

    def rows_of(first, height):
        sub, row = divmod(first, rows)
        index = []
        for axis, weight in region_dims:
            index.append(sub // weight % 2)
        return whole[tuple(index) + (slice(row, row + height), slice(None))]

    o_input, o_filter, o_mixing, o_output = outs
    unit, nodes = o_input.shape
    layers = o_filter.shape[0]
    scenarios = o_output.shape[1] // nodes
    for s in range(scenarios):
        o_output[:, s * nodes : (s + 1) * nodes] = rows_of(s * unit, unit)
    first = scenarios * unit
    for l in range(layers):
        for h in range(2):
            o_filter[l, :, h * nodes : (h + 1) * nodes] = rows_of(first + (l * 2 + h) * 2 * unit, 2 * unit)
        o_mixing[l] = rows_of(first + layers * 4 * unit + l * unit, unit)
    o_input[...] = rows_of(first + layers * 5 * unit, unit)


def reduce_grads(nt, nr, packed, grads, shapes):
    _, width, nodes = grads.shape
    rows = width // nr
    dims, tm_dims, region_dims, parts = plan(nt, nr, rows)
    grads = grads.reshape((2,) * len(dims) + (rows, nodes))
    whole = (2,) * len(region_dims) + (rows, nodes)
    if not packed:
        shapes = (whole,)
    vmem = pl.BlockSpec(memory_space=pltpu.VMEM)
    scratch = []
    for _, height, _ in parts:
        for phase in range(len(dims)):
            scratch.append(pltpu.VMEM((2,) * (len(dims) - phase - 1) + (height, nodes), BF16))
    copies = len(parts) * (len(dims) + len(region_dims))
    return pl.pallas_call(
        functools.partial(reduce_kernel, nt, nr, rows, packed, shapes),
        out_shape=tuple(jax.ShapeDtypeStruct(s, BF16) for s in shapes),
        in_specs=[vmem],
        out_specs=(vmem,) * len(shapes),
        scratch_shapes=scratch
        + [
            pltpu.VMEM(whole, BF16),
            pltpu.SemaphoreType.DMA((copies,)),
            pltpu.SemaphoreType.DMA((copies,)),
        ],
        compiler_params=pltpu.CompilerParams(
            collective_id=1, has_side_effects=True, vmem_limit_bytes=56 * 2**20
        ),
        name="reduce",
    )(grads)


def per_device(nt, nr, cov, obs, w_input, w_filter, w_mixing, w_output):
    nodes = cov.shape[2]
    weights = (w_input, w_filter, w_mixing, w_output)
    layers, channels = w_mixing.shape[:2]
    scenarios = w_output.shape[1] // nodes
    unit = channels // nt
    packed = unit % 16 == 0
    edges = exchange_edges(nt, cov, obs)
    cov_grad, *grads = run_network(nt, packed, cov, obs, edges, weights)
    shapes = (
        (unit, nodes), (layers, 2 * unit, 2 * channels), (layers, unit, channels), (unit, scenarios * nodes)
    )
    if packed:
        return (cov_grad,) + tuple(reduce_grads(nt, nr, True, grads[0], shapes))
    sources = tuple(
        jnp.moveaxis(g.reshape(g.shape[:-2] + (nt, -1) + g.shape[-1:]), -3, 0) for g in grads
    )
    flat = jnp.concatenate([s.reshape(nt, -1) for s in sources], axis=1).reshape(nt, -1, nodes)
    (summed,) = reduce_grads(nt, nr, False, flat, shapes)
    summed = summed.reshape(-1)
    outs, first = [], 0
    for source, shape in zip(sources, shapes):
        size = source.size // nt
        outs.append(summed[first : first + size].reshape(shape))
        first += size
    return (cov_grad, *outs)


def solution(mesh):
    placed = (P("region", "tm", None), P("region", "tm", None), P(), P(), P(), P())
    return jax.shard_map(
        functools.partial(per_device, mesh.shape["tm"], mesh.shape["region"]),
        mesh=mesh,
        in_specs=placed,
        out_specs=(
            P("region", "tm", None),
            P("tm", None),
            P(None, "tm", None),
            P(None, "tm", None),
            P("tm", None),
        ),
        check_vma=False,
    )
```

```python
import functools

import jax
import jax.numpy as jnp
from jax import lax
from jax.experimental import pallas as pl
from jax.experimental.pallas import tpu as pltpu
from jax.sharding import PartitionSpec as P

MESH = pl.DeviceIdType.MESH
epsilon = 1e-05
HALO = 8
F32 = jnp.float32
BF16 = jnp.bfloat16


def dot(a, b, ca=1, cb=0, precision=None):
    return lax.dot_general(
        a, b, (((ca,), (cb,)), ((), ())), precision=precision, preferred_element_type=F32
    )


def edges_kernel(
    nt, cov, obs, prev_cov, next_cov, next_obs, total,
    got_prev, got_next, got_obs, sums, send_sem, recv_sem,
):
    me = lax.axis_index("tm")
    rows = cov.shape[1]

    def at(offset):
        return {"tm": lax.rem(me + offset, nt)}

    barrier = pltpu.get_barrier_semaphore()
    for offset in range(1, nt):
        pl.semaphore_signal(barrier, inc=1, device_id=at(offset), device_id_type=MESH)
    sq = obs[...] * obs[...]
    seqs, _, nodes = obs.shape
    sq = jnp.sum(sq.reshape(seqs, rows // 8, 8, nodes), axis=1)
    own = sq[:, :, :128]
    for part in range(1, nodes // 128):
        own = own + sq[:, :, part * 128 : (part + 1) * 128]
    sums[0] = own
    pl.semaphore_wait(barrier, nt - 1)
    copies = []

    def send(src, dst, offset):
        slot = len(copies)
        copy = pltpu.make_async_remote_copy(
            src_ref=src, dst_ref=dst, send_sem=send_sem.at[slot], recv_sem=recv_sem.at[slot],
            device_id=at(offset), device_id_type=MESH,
        )
        copy.start()
        copies.append(copy)

    send(cov.at[:, pl.ds(rows - 16, 16), :], got_prev, 1)
    send(cov.at[:, pl.ds(0, 16), :], got_next, nt - 1)
    send(obs.at[:, pl.ds(0, HALO), :], got_obs, nt - 1)
    for offset in range(1, nt):
        send(sums.at[0], sums.at[offset], offset)
    for copy in copies:
        copy.wait()
    prev_cov[...] = got_prev[...]
    next_cov[...] = got_next[...]
    next_obs[...] = got_obs[...]
    total[...] = jnp.sum(sums[...], axis=0)


def exchange_edges(nt, cov, obs):
    seqs, rows, nodes = cov.shape
    vmem = pl.BlockSpec(memory_space=pltpu.VMEM)
    edge = jax.ShapeDtypeStruct((seqs, 16, nodes), BF16)
    copies = nt + 2
    return pl.pallas_call(
        functools.partial(edges_kernel, nt),
        out_shape=(
            edge,
            edge,
            jax.ShapeDtypeStruct((seqs, HALO, nodes), F32),
            jax.ShapeDtypeStruct((seqs, 8, 128), F32),
        ),
        in_specs=[vmem] * 2,
        out_specs=(vmem,) * 4,
        scratch_shapes=[
            pltpu.VMEM((seqs, 16, nodes), BF16),
            pltpu.VMEM((seqs, 16, nodes), BF16),
            pltpu.VMEM((seqs, HALO, nodes), F32),
            pltpu.VMEM((nt, seqs, 8, 128), F32),
            pltpu.SemaphoreType.DMA((copies,)),
            pltpu.SemaphoreType.DMA((copies,)),
        ],
        compiler_params=pltpu.CompilerParams(collective_id=0, has_side_effects=True),
        name="edges",
    )(cov, obs)


def network_kernel(
    nt, packed,
    cov, obs, prev_cov, next_cov, next_obs, total, w_input, w_filter, w_mixing, w_output,
    cov_grad, *rest,
):
    if packed:
        grads, scen, scored = rest
    else:
        g_input, g_filter, g_mixing, g_output, scen, scored = rest
    me = lax.axis_index("tm")
    seqs, rows, nodes = cov.shape
    layers = w_filter.shape[0]
    channels = w_mixing.shape[1]
    scenarios = w_output.shape[1] // nodes
    span = rows + 2 * HALO
    kept = rows + HALO
    unit = channels // nt
    not_first = (me > 0).astype(F32)
    not_last = (me < nt - 1).astype(F32)

    def own_rows(x):
        return jnp.concatenate([x[b * span + HALO : b * span + HALO + rows] for b in range(seqs)], axis=0)

    def put(first_row, height, value):
        grads[:, first_row : first_row + height, :] = value.reshape(nt, height, nodes).astype(BF16)

    cov_own = cov[...]
    spans = []
    for b in range(seqs):
        spans.append(prev_cov[b].astype(F32)[16 - HALO :] * not_first)
        spans.append(cov_own[b].astype(F32))
        spans.append(next_cov[b].astype(F32)[:HALO])
    hidden = dot(jnp.concatenate(spans, axis=0).astype(BF16), w_input[...]).astype(BF16).astype(F32)
    stored = []
    for l in range(layers):
        delayed = pltpu.roll(hidden, 2**l, 0)
        joined = jnp.concatenate([delayed, hidden], axis=1).astype(BF16)
        preact = dot(joined, w_filter[l])
        act = jnp.tanh(preact[:, :channels])
        gate = 0.5 * jnp.tanh(0.5 * preact[:, channels:]) + 0.5
        gated = (act * gate).astype(BF16)
        stored.append((delayed, hidden, act, gate))
        hidden = (hidden + dot(gated, w_mixing[l])).astype(BF16).astype(F32)

    last = jnp.concatenate([hidden[b * span + HALO : (b + 1) * span] for b in range(seqs)], axis=0)
    last = last.astype(BF16)
    for s in range(scenarios):
        pred = dot(last, w_output[:, s * nodes : (s + 1) * nodes])
        for half in range(nodes // 128):
            scen[half, pl.ds(s, seqs * kept, stride=scenarios), :] = pred[:, half * 128 : (half + 1) * 128]
    for b in range(seqs):
        scored[b * kept : b * kept + rows] = obs[b]
        scored[b * kept + rows : (b + 1) * kept] = next_obs[b]

    block = 16 * scenarios
    row_no = lax.broadcasted_iota(jnp.int32, (block, block), 0)
    col_no = lax.broadcasted_iota(jnp.int32, (block, block), 1)
    same_step = (row_no // scenarios) == (col_no // scenarios)
    diagonal = row_no == col_no
    pairs = jnp.where(same_step & ~diagonal, 1.0 / (scenarios * (scenarios - 1) * nodes), 0.0)
    halves = nodes // 128

    def score(groups):
        ats = [pl.ds(pl.multiple_of(g * block, block), block) for g in groups]
        ys = [jnp.concatenate([scen[h, at, :] for h in range(halves)], axis=1) for at in ats]
        highs = [y.astype(BF16) for y in ys]
        lows = [(y - hi.astype(F32)).astype(BF16) for y, hi in zip(ys, highs)]
        grams = [
            dot(jnp.concatenate([hi, lo, hi, lo], axis=1), jnp.concatenate([hi, hi, lo, lo], axis=1), 1, 1)
            for hi, lo in zip(highs, lows)
        ]
        targets = []
        for g, y in zip(groups, ys):
            o = scored[pl.ds(pl.multiple_of(g * 16, 16), 16), :]
            diff = y - jnp.broadcast_to(o[:, None, :], (16, scenarios, nodes)).reshape(block, nodes)
            inv = lax.rsqrt(jnp.sum(diff * diff, axis=1, keepdims=True) * (1.0 / nodes) + epsilon)
            targets.append(inv * (1.0 / (scenarios * nodes)) * diff)
        coefs = []
        for gram in grams:
            own = jnp.where(diagonal, gram, 0.0)
            own_sq = jnp.sum(own, axis=1, keepdims=True) + jnp.sum(own, axis=0, keepdims=True)
            pair_sq = jnp.maximum(own_sq - 2.0 * gram, 0.0) * (1.0 / nodes)
            coefs.append(pairs * lax.rsqrt(pair_sq + epsilon))
        for at, y, hi, lo, coef, target in zip(ats, ys, highs, lows, coefs, targets):
            chi = coef.astype(BF16)
            clo = (coef - chi.astype(F32)).astype(BF16)
            mixed = dot(jnp.concatenate([chi, clo, chi], axis=1), jnp.concatenate([hi, hi, lo], axis=0))
            grad = mixed - jnp.sum(coef, axis=1, keepdims=True) * y + target
            for h in range(halves):
                scen[h, at, :] = grad[:, h * 128 : (h + 1) * 128]

    groups = seqs * kept // 16

    def score_pair(i, carry):
        score([2 * i, 2 * i + 1])
        return carry

    lax.fori_loop(0, groups // 2, score_pair, 0)
    if groups % 2:
        score([groups - 1])

    length = rows * nt
    step_no = lax.broadcasted_iota(jnp.int32, (kept, 1), 0)
    valid = jnp.where(step_no < rows, 1.0, not_last)
    factor = []
    for b in range(seqs):
        sq = jnp.sum(jnp.sum(total[b], axis=1, keepdims=True), axis=0, keepdims=True)
        factor.append(valid * lax.rsqrt(sq / (length * nodes) + epsilon))
    factor = jnp.concatenate(factor, axis=0)

    def kept_own(x):
        return jnp.concatenate([x[b * kept : b * kept + rows] for b in range(seqs)], axis=0)

    last_own = own_rows(hidden).T.astype(BF16)
    grad_last = jnp.zeros((seqs * kept, channels), F32)
    for s in range(scenarios):
        g = jnp.concatenate(
            [scen[h, pl.ds(s, seqs * kept, stride=scenarios), :] for h in range(halves)], axis=1
        )
        g = g * factor
        grad_last = grad_last + dot(g.astype(BF16), w_output[:, s * nodes : (s + 1) * nodes], 1, 1)
        part = dot(last_own, kept_own(g).astype(BF16))
        if packed:
            put(s * unit, unit, part)
        else:
            g_output[:, s * nodes : (s + 1) * nodes] = part.astype(BF16)
    grad_last = grad_last.astype(BF16).astype(F32)
    pieces = []
    for b in range(seqs):
        pieces.append(jnp.zeros((HALO, channels), F32))
        pieces.append(grad_last[b * kept : (b + 1) * kept])
    grad = jnp.concatenate(pieces, axis=0)

    first = scenarios * unit
    for l in reversed(range(layers)):
        delayed, held, act, gate = stored[l]
        grad16 = grad.astype(BF16)
        gated_t = own_rows(act * gate).T.astype(BF16)
        part = dot(gated_t, own_rows(grad).astype(BF16))
        if packed:
            put(first + layers * 4 * unit + l * unit, unit, part)
        else:
            g_mixing[l] = part.astype(BF16)
        gated_cot = dot(grad16, w_mixing[l], 1, 1).astype(BF16).astype(F32)
        pre = jnp.concatenate(
            [gated_cot * gate * (1.0 - act * act), gated_cot * act * gate * (1.0 - gate)], axis=1
        )
        own_pre = own_rows(pre).astype(BF16)
        for tap, source in enumerate((delayed, held)):
            part = dot(own_rows(source).T.astype(BF16), own_pre)
            if packed:
                owners = nt // 2
                height = 2 * unit
                for half in range(2):
                    piece = part[:, half * nodes : (half + 1) * nodes].reshape(owners, height, nodes)
                    at = first + (l * 2 + half) * height
                    grads[tap * owners : (tap + 1) * owners, at : at + height, :] = piece.astype(BF16)
            else:
                g_filter[l, tap * channels : (tap + 1) * channels, :] = part.astype(BF16)
        both = dot(pre.astype(BF16), w_filter[l], 1, 1).astype(BF16).astype(F32)
        past = pltpu.roll(both[:, :channels], seqs * span - 2**l, 0)
        grad = (grad + both[:, channels:] + past).astype(BF16).astype(F32)

    own = own_rows(grad).astype(BF16)
    cov_flat = jnp.concatenate([cov_own[b] for b in range(seqs)], axis=0)
    part = dot(cov_flat.astype(F32).T.astype(BF16), own)
    if packed:
        put(first + layers * 5 * unit, unit, part)
    else:
        g_input[...] = part.astype(BF16)
    result = dot(own, w_input[...], 1, 1).astype(BF16)
    for b in range(seqs):
        cov_grad[b] = result[b * rows : (b + 1) * rows]


def run_network(nt, packed, cov, obs, edges, weights):
    seqs, rows, nodes = cov.shape
    w_input, w_filter, w_mixing, w_output = weights
    scenarios = w_output.shape[1] // nodes
    vmem = pl.BlockSpec(memory_space=pltpu.VMEM)
    if packed:
        width = sum(w.size for w in weights) // nt // nodes
        grads = (jax.ShapeDtypeStruct((nt, width, nodes), BF16),)
    else:
        grads = tuple(jax.ShapeDtypeStruct(w.shape, BF16) for w in weights)
    steps = seqs * (rows + HALO)
    return pl.pallas_call(
        functools.partial(network_kernel, nt, packed),
        out_shape=(jax.ShapeDtypeStruct(cov.shape, BF16),) + grads,
        in_specs=[vmem] * 10,
        out_specs=(vmem,) * (1 + len(grads)),
        scratch_shapes=[
            pltpu.VMEM((nodes // 128, steps * scenarios, 128), F32),
            pltpu.VMEM((steps, nodes), F32),
        ],
        compiler_params=pltpu.CompilerParams(vmem_limit_bytes=56 * 2**20),
        name="network",
    )(cov, obs, *edges, *weights)


def plan(nt, nr, rows):
    bits = lambda n: n.bit_length() - 1
    tm_dims = [("tm", 2**i) for i in reversed(range(bits(nt)))]
    region_dims = [("region", 2**i) for i in reversed(range(bits(nr)))]
    near = region_dims[-1:]
    x, ys = region_dims[:-1], list(reversed(tm_dims))
    y, z = ys[:1], ys[1:]
    orders = [near + x + y + z, near + y + z[:1] + x + z[1:], near + z[:1] + x + y + z[1:]]
    units = rows // 16
    count = min(2 * len(orders), units)
    cuts = [16 * (units * i // count) for i in range(count + 1)]
    parts = [(cuts[i], cuts[i + 1] - cuts[i], orders[i % 3]) for i in range(count)]
    return tm_dims + region_dims, tm_dims, region_dims, parts


def reduce_kernel(nt, nr, rows, grads, out, *refs):
    dims, tm_dims, region_dims, parts = plan(nt, nr, rows)
    send_sem, recv_sem = refs[-2:]
    whole = refs[-3]
    where = {"tm": lax.axis_index("tm"), "region": lax.axis_index("region")}

    def bit(dim):
        axis, weight = dim
        return lax.rem(lax.div(where[axis], weight), 2)

    def across(dim):
        axis, weight = dim
        return {axis: where[axis] + weight * (1 - 2 * bit(dim))}

    barrier = pltpu.get_barrier_semaphore()
    for dim in dims:
        pl.semaphore_signal(barrier, inc=1, device_id=across(dim), device_id_type=MESH)
    pl.semaphore_wait(barrier, len(dims))

    slot = 0
    state = []
    for i, (start, height, order) in enumerate(parts):
        buffers = refs[i * len(dims) : (i + 1) * len(dims)]
        state.append([grads, list(dims), buffers])

    def start_copy(src, dst, dim):
        nonlocal slot
        copy = pltpu.make_async_remote_copy(
            src_ref=src, dst_ref=dst, send_sem=send_sem.at[slot], recv_sem=recv_sem.at[slot],
            device_id=across(dim), device_id_type=MESH,
        )
        slot += 1
        copy.start()
        return copy

    def half(i, dim, side):
        left = state[i][1]
        rows_at = pl.ds(parts[i][0], parts[i][1]) if state[i][0] is grads else slice(None)
        return tuple(side if d == dim else slice(None) for d in left) + (rows_at, slice(None))

    def send_half(i, phase):
        dim = parts[i][2][phase]
        return start_copy(state[i][0].at[half(i, dim, 1 - bit(dim))], state[i][2][phase], dim)

    def gather_at(dim):
        place = region_dims.index(dim)
        return tuple(bit(d) if n <= place else slice(None) for n, d in enumerate(region_dims))

    def send_whole(i, n):
        dim = list(region_dims)[n]
        index = tuple(slice(None) if m < n else bit(d) for m, d in enumerate(region_dims))
        index = index + (pl.ds(parts[i][0], parts[i][1]), slice(None))
        return start_copy(whole.at[index], whole.at[index], dim)

    flying = [send_half(i, 0) for i in range(len(parts))]
    done = []
    for phase in range(len(dims)):
        for i in range(len(parts)):
            dim = parts[i][2][phase]
            flying[i].wait_recv()
            done.append(flying[i])
            source, left, buffers = state[i]
            into = buffers[phase]
            mine = source[half(i, dim, bit(dim))]
            into[...] = (into[...].astype(F32) + mine.astype(F32)).astype(BF16)
            state[i][0] = into
            state[i][1] = [d for d in left if d != dim]
            if phase + 1 < len(dims):
                flying[i] = send_half(i, phase + 1)
            else:
                index = tuple(bit(d) for d in region_dims)
                whole[index + (pl.ds(parts[i][0], parts[i][1]), slice(None))] = into[...]
                flying[i] = send_whole(i, 0)
    for n in range(len(region_dims)):
        for i in range(len(parts)):
            flying[i].wait_recv()
            done.append(flying[i])
            if n + 1 < len(region_dims):
                flying[i] = send_whole(i, n + 1)
    for copy in done:
        copy.wait_send()

    out[...] = whole[...]


def unpack_kernel(rows, whole, o_input, o_filter, o_mixing, o_output):
    def rows_of(first, height):
        sub, row = divmod(first, rows)
        return whole[sub, row : row + height, :]

    unit, nodes = o_input.shape
    layers = o_filter.shape[0]
    scenarios = o_output.shape[1] // nodes
    for s in range(scenarios):
        o_output[:, s * nodes : (s + 1) * nodes] = rows_of(s * unit, unit)
    first = scenarios * unit
    for l in range(layers):
        for h in range(2):
            o_filter[l, :, h * nodes : (h + 1) * nodes] = rows_of(first + (l * 2 + h) * 2 * unit, 2 * unit)
        o_mixing[l] = rows_of(first + layers * 4 * unit + l * unit, unit)
    o_input[...] = rows_of(first + layers * 5 * unit, unit)


def reduce_grads(nt, nr, grads):
    _, width, nodes = grads.shape
    rows = width // nr
    dims, tm_dims, region_dims, parts = plan(nt, nr, rows)
    grads = grads.reshape((2,) * len(dims) + (rows, nodes))
    whole = (2,) * len(region_dims) + (rows, nodes)
    vmem = pl.BlockSpec(memory_space=pltpu.VMEM)
    scratch = []
    for _, height, _ in parts:
        for phase in range(len(dims)):
            scratch.append(pltpu.VMEM((2,) * (len(dims) - phase - 1) + (height, nodes), BF16))
    copies = len(parts) * (len(dims) + len(region_dims))
    return pl.pallas_call(
        functools.partial(reduce_kernel, nt, nr, rows),
        out_shape=jax.ShapeDtypeStruct(whole, BF16),
        in_specs=[vmem],
        out_specs=vmem,
        scratch_shapes=scratch
        + [
            pltpu.VMEM(whole, BF16),
            pltpu.SemaphoreType.DMA((copies,)),
            pltpu.SemaphoreType.DMA((copies,)),
        ],
        compiler_params=pltpu.CompilerParams(
            collective_id=1, has_side_effects=True, vmem_limit_bytes=56 * 2**20
        ),
        name="reduce",
    )(grads).reshape(nr, rows, nodes)


def unpack(summed, shapes):
    vmem = pl.BlockSpec(memory_space=pltpu.VMEM)
    return pl.pallas_call(
        functools.partial(unpack_kernel, summed.shape[1]),
        out_shape=tuple(jax.ShapeDtypeStruct(s, BF16) for s in shapes),
        in_specs=[vmem],
        out_specs=(vmem,) * len(shapes),
        name="unpack",
    )(summed)


def per_device(nt, nr, cov, obs, w_input, w_filter, w_mixing, w_output):
    nodes = cov.shape[2]
    weights = (w_input, w_filter, w_mixing, w_output)
    layers, channels = w_mixing.shape[:2]
    scenarios = w_output.shape[1] // nodes
    unit = channels // nt
    packed = unit % 16 == 0
    edges = exchange_edges(nt, cov, obs)
    cov_grad, *grads = run_network(nt, packed, cov, obs, edges, weights)
    shapes = (
        (unit, nodes), (layers, 2 * unit, 2 * channels), (layers, unit, channels), (unit, scenarios * nodes)
    )
    if packed:
        return (cov_grad, *unpack(reduce_grads(nt, nr, grads[0]), shapes))
    sources = tuple(
        jnp.moveaxis(g.reshape(g.shape[:-2] + (nt, -1) + g.shape[-1:]), -3, 0) for g in grads
    )
    flat = jnp.concatenate([s.reshape(nt, -1) for s in sources], axis=1).reshape(nt, -1, nodes)
    summed = reduce_grads(nt, nr, flat).reshape(-1)
    outs, first = [], 0
    for source, shape in zip(sources, shapes):
        size = source.size // nt
        outs.append(summed[first : first + size].reshape(shape))
        first += size
    return (cov_grad, *outs)


def solution(mesh):
    placed = (P("region", "tm", None), P("region", "tm", None), P(), P(), P(), P())
    return jax.shard_map(
        functools.partial(per_device, mesh.shape["tm"], mesh.shape["region"]),
        mesh=mesh,
        in_specs=placed,
        out_specs=(
            P("region", "tm", None),
            P("tm", None),
            P(None, "tm", None),
            P(None, "tm", None),
            P("tm", None),
        ),
        check_vma=False,
    )
```

```python
import functools

import jax
import jax.numpy as jnp
from jax import lax
from jax.experimental import pallas as pl
from jax.experimental.pallas import tpu as pltpu
from jax.sharding import PartitionSpec as P

MESH = pl.DeviceIdType.MESH
epsilon = 1e-05
HALO = 8
F32 = jnp.float32
BF16 = jnp.bfloat16


def dot(a, b, ca=1, cb=0, precision=None):
    return lax.dot_general(
        a, b, (((ca,), (cb,)), ((), ())), precision=precision, preferred_element_type=F32
    )


class Edges:
    def __init__(self, nt, cov, obs, got_prev, got_next, got_obs, sums, send_sem, recv_sem):
        self.nt, self.cov, self.obs, self.sums = nt, cov, obs, sums
        self.got = (got_prev, got_next, got_obs)
        self.send_sem, self.recv_sem = send_sem, recv_sem
        self.copies = []

    def at(self, offset):
        return {"tm": lax.rem(lax.axis_index("tm") + offset, self.nt)}

    def greet(self, barrier):
        for offset in range(1, self.nt):
            pl.semaphore_signal(barrier, inc=1, device_id=self.at(offset), device_id_type=MESH)

    def own_squares(self):
        seqs, rows, nodes = self.obs.shape
        sq = self.obs[...] * self.obs[...]
        sq = jnp.sum(sq.reshape(seqs, rows // 8, 8, nodes), axis=1)
        own = sq[:, :, :128]
        for part in range(1, nodes // 128):
            own = own + sq[:, :, part * 128 : (part + 1) * 128]
        self.sums[0] = own

    def send(self, src, dst, offset):
        slot = len(self.copies)
        copy = pltpu.make_async_remote_copy(
            src_ref=src, dst_ref=dst,
            send_sem=self.send_sem.at[slot], recv_sem=self.recv_sem.at[slot],
            device_id=self.at(offset), device_id_type=MESH,
        )
        copy.start()
        self.copies.append(copy)

    def start(self):
        nt, rows = self.nt, self.cov.shape[1]
        self.send(self.cov.at[:, pl.ds(rows - 16, 16), :], self.got[0], 1)
        self.send(self.cov.at[:, pl.ds(0, 16), :], self.got[1], nt - 1)
        self.send(self.obs.at[:, pl.ds(0, HALO), :], self.got[2], nt - 1)
        for offset in range(1, nt):
            self.send(self.sums.at[0], self.sums.at[offset], offset)

    def arrived(self, first, last):
        for copy in self.copies[first:last]:
            copy.wait_recv()

    def sent(self):
        for copy in self.copies:
            copy.wait_send()

    def total(self):
        return jnp.sum(self.sums[...], axis=0)


def edges_kernel(nt, cov, obs, prev_cov, next_cov, next_obs, total, *scratch):
    edges = Edges(nt, cov, obs, *scratch)
    barrier = pltpu.get_barrier_semaphore()
    edges.greet(barrier)
    edges.own_squares()
    pl.semaphore_wait(barrier, nt - 1)
    edges.start()
    edges.arrived(0, None)
    edges.sent()
    for out, got in zip((prev_cov, next_cov, next_obs), edges.got):
        out[...] = got[...]
    total[...] = edges.total()


def exchange_edges(nt, cov, obs):
    seqs, rows, nodes = cov.shape
    vmem = pl.BlockSpec(memory_space=pltpu.VMEM)
    edge = jax.ShapeDtypeStruct((seqs, 16, nodes), BF16)
    copies = nt + 2
    return pl.pallas_call(
        functools.partial(edges_kernel, nt),
        out_shape=(
            edge,
            edge,
            jax.ShapeDtypeStruct((seqs, HALO, nodes), F32),
            jax.ShapeDtypeStruct((seqs, 8, 128), F32),
        ),
        in_specs=[vmem] * 2,
        out_specs=(vmem,) * 4,
        scratch_shapes=[
            pltpu.VMEM((seqs, 16, nodes), BF16),
            pltpu.VMEM((seqs, 16, nodes), BF16),
            pltpu.VMEM((seqs, HALO, nodes), F32),
            pltpu.VMEM((nt, seqs, 8, 128), F32),
            pltpu.SemaphoreType.DMA((copies,)),
            pltpu.SemaphoreType.DMA((copies,)),
        ],
        compiler_params=pltpu.CompilerParams(collective_id=0, has_side_effects=True),
        name="edges",
    )(cov, obs)


def network(
    nt, cov, obs, prev_cov, next_cov, next_obs, w_input, w_filter, w_mixing, w_output,
    cov_grad, scen, scored, need, emit, after,
):
    me = lax.axis_index("tm")
    seqs, rows, nodes = cov.shape
    layers = w_filter.shape[0]
    channels = w_mixing.shape[1]
    scenarios = w_output.shape[1] // nodes
    span = rows + 2 * HALO
    kept = rows + HALO
    not_first = (me > 0).astype(F32)
    not_last = (me < nt - 1).astype(F32)

    def own_rows(x):
        return jnp.concatenate([x[b * span + HALO : b * span + HALO + rows] for b in range(seqs)], axis=0)

    cov_own = cov[...]
    need("cov")
    need("input")
    spans = []
    for b in range(seqs):
        spans.append(prev_cov[b].astype(F32)[16 - HALO :] * not_first)
        spans.append(cov_own[b].astype(F32))
        spans.append(next_cov[b].astype(F32)[:HALO])
    hidden = dot(jnp.concatenate(spans, axis=0).astype(BF16), w_input[...]).astype(BF16).astype(F32)
    stored = []
    need("filter")
    need("mixing")
    for l in range(layers):
        delayed = pltpu.roll(hidden, 2**l, 0)
        joined = jnp.concatenate([delayed, hidden], axis=1).astype(BF16)
        preact = dot(joined, w_filter[l])
        act = jnp.tanh(preact[:, :channels])
        gate = 0.5 * jnp.tanh(0.5 * preact[:, channels:]) + 0.5
        gated = (act * gate).astype(BF16)
        stored.append((delayed, hidden, act, gate))
        hidden = (hidden + dot(gated, w_mixing[l])).astype(BF16).astype(F32)

    last = jnp.concatenate([hidden[b * span + HALO : (b + 1) * span] for b in range(seqs)], axis=0)
    last = last.astype(BF16)
    need("output")
    for s in range(scenarios):
        pred = dot(last, w_output[:, s * nodes : (s + 1) * nodes])
        for half in range(nodes // 128):
            scen[half, pl.ds(s, seqs * kept, stride=scenarios), :] = pred[:, half * 128 : (half + 1) * 128]
    need("obs")
    for b in range(seqs):
        scored[b * kept : b * kept + rows] = obs[b]
        scored[b * kept + rows : (b + 1) * kept] = next_obs[b]

    block = 16 * scenarios
    row_no = lax.broadcasted_iota(jnp.int32, (block, block), 0)
    col_no = lax.broadcasted_iota(jnp.int32, (block, block), 1)
    same_step = (row_no // scenarios) == (col_no // scenarios)
    diagonal = row_no == col_no
    pairs = jnp.where(same_step & ~diagonal, 1.0 / (scenarios * (scenarios - 1) * nodes), 0.0)
    halves = nodes // 128

    def score(groups):
        ats = [pl.ds(pl.multiple_of(g * block, block), block) for g in groups]
        ys = [jnp.concatenate([scen[h, at, :] for h in range(halves)], axis=1) for at in ats]
        highs = [y.astype(BF16) for y in ys]
        lows = [(y - hi.astype(F32)).astype(BF16) for y, hi in zip(ys, highs)]
        grams = [
            dot(jnp.concatenate([hi, lo, hi, lo], axis=1), jnp.concatenate([hi, hi, lo, lo], axis=1), 1, 1)
            for hi, lo in zip(highs, lows)
        ]
        targets = []
        for g, y in zip(groups, ys):
            o = scored[pl.ds(pl.multiple_of(g * 16, 16), 16), :]
            diff = y - jnp.broadcast_to(o[:, None, :], (16, scenarios, nodes)).reshape(block, nodes)
            inv = lax.rsqrt(jnp.sum(diff * diff, axis=1, keepdims=True) * (1.0 / nodes) + epsilon)
            targets.append(inv * (1.0 / (scenarios * nodes)) * diff)
        coefs = []
        for gram in grams:
            own = jnp.where(diagonal, gram, 0.0)
            own_sq = jnp.sum(own, axis=1, keepdims=True) + jnp.sum(own, axis=0, keepdims=True)
            pair_sq = jnp.maximum(own_sq - 2.0 * gram, 0.0) * (1.0 / nodes)
            coefs.append(pairs * lax.rsqrt(pair_sq + epsilon))
        for at, y, hi, lo, coef, target in zip(ats, ys, highs, lows, coefs, targets):
            chi = coef.astype(BF16)
            clo = (coef - chi.astype(F32)).astype(BF16)
            mixed = dot(jnp.concatenate([chi, clo, chi], axis=1), jnp.concatenate([hi, hi, lo], axis=0))
            grad = mixed - jnp.sum(coef, axis=1, keepdims=True) * y + target
            for h in range(halves):
                scen[h, at, :] = grad[:, h * 128 : (h + 1) * 128]

    groups = seqs * kept // 16

    def score_pair(i, carry):
        score([2 * i, 2 * i + 1])
        return carry

    lax.fori_loop(0, groups // 2, score_pair, 0)
    if groups % 2:
        score([groups - 1])

    length = rows * nt
    step_no = lax.broadcasted_iota(jnp.int32, (kept, 1), 0)
    valid = jnp.where(step_no < rows, 1.0, not_last)
    factor = []
    total = need("total")
    for b in range(seqs):
        sq = jnp.sum(jnp.sum(total[b], axis=1, keepdims=True), axis=0, keepdims=True)
        factor.append(valid * lax.rsqrt(sq / (length * nodes) + epsilon))
    factor = jnp.concatenate(factor, axis=0)

    def kept_own(x):
        return jnp.concatenate([x[b * kept : b * kept + rows] for b in range(seqs)], axis=0)

    last_own = own_rows(hidden).T.astype(BF16)
    grad_last = jnp.zeros((seqs * kept, channels), F32)
    for s in range(scenarios):
        g = jnp.concatenate(
            [scen[h, pl.ds(s, seqs * kept, stride=scenarios), :] for h in range(halves)], axis=1
        )
        g = g * factor
        grad_last = grad_last + dot(g.astype(BF16), w_output[:, s * nodes : (s + 1) * nodes], 1, 1)
        part = dot(last_own, kept_own(g).astype(BF16))
        emit("output", s, part)
    after("output")
    grad_last = grad_last.astype(BF16).astype(F32)
    pieces = []
    for b in range(seqs):
        pieces.append(jnp.zeros((HALO, channels), F32))
        pieces.append(grad_last[b * kept : (b + 1) * kept])
    grad = jnp.concatenate(pieces, axis=0)

    for l in reversed(range(layers)):
        delayed, held, act, gate = stored[l]
        grad16 = grad.astype(BF16)
        gated_t = own_rows(act * gate).T.astype(BF16)
        part = dot(gated_t, own_rows(grad).astype(BF16))
        emit("mixing", l, part)
        gated_cot = dot(grad16, w_mixing[l], 1, 1).astype(BF16).astype(F32)
        pre = jnp.concatenate(
            [gated_cot * gate * (1.0 - act * act), gated_cot * act * gate * (1.0 - gate)], axis=1
        )
        own_pre = own_rows(pre).astype(BF16)
        for tap, source in enumerate((delayed, held)):
            part = dot(own_rows(source).T.astype(BF16), own_pre)
            emit("filter", (l, tap), part)
        after(l)
        both = dot(pre.astype(BF16), w_filter[l], 1, 1).astype(BF16).astype(F32)
        past = pltpu.roll(both[:, :channels], seqs * span - 2**l, 0)
        grad = (grad + both[:, channels:] + past).astype(BF16).astype(F32)

    own = own_rows(grad).astype(BF16)
    cov_flat = jnp.concatenate([cov_own[b] for b in range(seqs)], axis=0)
    part = dot(cov_flat.astype(F32).T.astype(BF16), own)
    emit("input", None, part)
    after("input")
    result = dot(own, w_input[...], 1, 1).astype(BF16)
    for b in range(seqs):
        cov_grad[b] = result[b * rows : (b + 1) * rows]


def network_kernel(nt, cov, obs, prev_cov, next_cov, next_obs, total, *rest):
    weights, cov_grad, grads, (scen, scored) = rest[:4], rest[4], rest[5:9], rest[9:]
    g_input, g_filter, g_mixing, g_output = grads
    nodes, channels = cov.shape[2], weights[2].shape[1]

    def need(name):
        return total[...] if name == "total" else None

    def emit(name, index, part):
        part = part.astype(BF16)
        if name == "output":
            g_output[:, index * nodes : (index + 1) * nodes] = part
        elif name == "mixing":
            g_mixing[index] = part
        elif name == "filter":
            l, tap = index
            g_filter[l, tap * channels : (tap + 1) * channels, :] = part
        else:
            g_input[...] = part

    network(
        nt, cov, obs, prev_cov, next_cov, next_obs, *weights, cov_grad, scen, scored,
        need, emit, lambda stage: None,
    )


def network_scratch(cov, w_output):
    seqs, rows, nodes = cov.shape
    steps = seqs * (rows + HALO)
    scenarios = w_output.shape[1] // nodes
    return [
        pltpu.VMEM((nodes // 128, steps * scenarios, 128), F32),
        pltpu.VMEM((steps, nodes), F32),
    ]


def run_network(nt, cov, obs, edges, weights):
    vmem = pl.BlockSpec(memory_space=pltpu.VMEM)
    grads = tuple(jax.ShapeDtypeStruct(w.shape, BF16) for w in weights)
    return pl.pallas_call(
        functools.partial(network_kernel, nt),
        out_shape=(jax.ShapeDtypeStruct(cov.shape, BF16),) + grads,
        in_specs=[vmem] * 10,
        out_specs=(vmem,) * (1 + len(grads)),
        scratch_shapes=network_scratch(cov, weights[3]),
        compiler_params=pltpu.CompilerParams(vmem_limit_bytes=56 * 2**20),
        name="network",
    )(cov, obs, *edges, *weights)


def bit_dims(nt, nr):
    bits = lambda n: n.bit_length() - 1
    tm_dims = [("tm", 2**i) for i in reversed(range(bits(nt)))]
    region_dims = [("region", 2**i) for i in reversed(range(bits(nr)))]
    return tm_dims, region_dims


def orders_of(tm_dims, region_dims):
    near = region_dims[-1:]
    x, ys = region_dims[:-1], list(reversed(tm_dims))
    y, z = ys[:1], ys[1:]
    return [near + x + y + z, near + y + z[:1] + x + z[1:], near + z[:1] + x + y + z[1:]]


def even_parts(rows, orders):
    units = rows // 16
    count = min(2 * len(orders), units)
    cuts = [16 * (units * i // count) for i in range(count + 1)]
    return [(cuts[i], cuts[i + 1] - cuts[i], orders[i % 3]) for i in range(count)]


class Halving:
    def __init__(self, source, tm_dims, region_dims, parts, buffers, whole, send_sem, recv_sem):
        self.dims, self.region_dims, self.parts = tm_dims + region_dims, region_dims, parts
        self.source, self.whole = source, whole
        self.send_sem, self.recv_sem = send_sem, recv_sem
        n = len(self.dims)
        self.buffers = [buffers[i * n : (i + 1) * n] for i in range(len(parts))]
        self.current = [source for _ in parts]
        self.left = [list(self.dims) for _ in parts]
        self.phase = [0 for _ in parts]
        self.flying = [None for _ in parts]
        self.done = []
        self.slot = 0
        self.where = {"tm": lax.axis_index("tm"), "region": lax.axis_index("region")}

    def bit(self, dim):
        axis, weight = dim
        return lax.rem(lax.div(self.where[axis], weight), 2)

    def across(self, dim):
        axis, weight = dim
        return {axis: self.where[axis] + weight * (1 - 2 * self.bit(dim))}

    def copy(self, i, src, dst, dim):
        copy = pltpu.make_async_remote_copy(
            src_ref=src, dst_ref=dst,
            send_sem=self.send_sem.at[self.slot], recv_sem=self.recv_sem.at[self.slot],
            device_id=self.across(dim), device_id_type=MESH,
        )
        self.slot += 1
        copy.start()
        self.flying[i] = copy

    def rows_at(self, i):
        return pl.ds(self.parts[i][0], self.parts[i][1])

    def half(self, i, dim, side):
        rows = self.rows_at(i) if self.phase[i] == 0 else slice(None)
        return tuple(side if d == dim else slice(None) for d in self.left[i]) + (rows, slice(None))

    def send_half(self, i):
        dim = self.parts[i][2][self.phase[i]]
        at = self.half(i, dim, 1 - self.bit(dim))
        self.copy(i, self.current[i].at[at], self.buffers[i][self.phase[i]], dim)

    def send_whole(self, i, n):
        index = tuple(slice(None) if m < n else self.bit(d) for m, d in enumerate(self.region_dims))
        index = index + (self.rows_at(i), slice(None))
        self.copy(i, self.whole.at[index], self.whole.at[index], self.region_dims[n])

    def begin(self, i):
        self.send_half(i)

    def advance(self, i):
        if self.flying[i] is None:
            return False
        self.flying[i].wait_recv()
        self.done.append(self.flying[i])
        self.flying[i] = None
        phase, last = self.phase[i], len(self.dims)
        if phase < last:
            dim = self.parts[i][2][phase]
            into = self.buffers[i][phase]
            mine = self.current[i][self.half(i, dim, self.bit(dim))]
            into[...] = (into[...].astype(F32) + mine.astype(F32)).astype(BF16)
            self.current[i] = into
            self.left[i] = [d for d in self.left[i] if d != dim]
            self.phase[i] += 1
            if phase + 1 < last:
                self.send_half(i)
            else:
                index = tuple(self.bit(d) for d in self.region_dims)
                self.whole[index + (self.rows_at(i), slice(None))] = into[...]
                self.send_whole(i, 0)
        else:
            self.phase[i] += 1
            if phase + 1 - last < len(self.region_dims):
                self.send_whole(i, phase + 1 - last)
        return True

    def round(self):
        return any([self.advance(i) for i in range(len(self.parts))])

    def finish(self):
        while self.round():
            pass
        for copy in self.done:
            copy.wait_send()


def halving_scratch(tm_dims, region_dims, parts, rows, nodes):
    n = len(tm_dims) + len(region_dims)
    scratch = []
    for _, height, _ in parts:
        for phase in range(n):
            scratch.append(pltpu.VMEM((2,) * (n - phase - 1) + (height, nodes), BF16))
    copies = len(parts) * (n + len(region_dims))
    return scratch, [
        pltpu.VMEM((2,) * len(region_dims) + (rows, nodes), BF16),
        pltpu.SemaphoreType.DMA((copies,)),
        pltpu.SemaphoreType.DMA((copies,)),
    ]


def reduce_kernel(tm_dims, region_dims, parts, grads, out, *refs):
    halving = Halving(grads, tm_dims, region_dims, parts, refs[:-3], *refs[-3:])
    barrier = pltpu.get_barrier_semaphore()
    for dim in halving.dims:
        pl.semaphore_signal(barrier, inc=1, device_id=halving.across(dim), device_id_type=MESH)
    pl.semaphore_wait(barrier, len(halving.dims))
    for i in range(len(parts)):
        halving.begin(i)
    halving.finish()
    out[...] = halving.whole[...]


def reduce_grads(nt, nr, grads):
    _, width, nodes = grads.shape
    rows = width // nr
    tm_dims, region_dims = bit_dims(nt, nr)
    parts = even_parts(rows, orders_of(tm_dims, region_dims))
    grads = grads.reshape((2,) * (len(tm_dims) + len(region_dims)) + (rows, nodes))
    buffers, ends = halving_scratch(tm_dims, region_dims, parts, rows, nodes)
    vmem = pl.BlockSpec(memory_space=pltpu.VMEM)
    return pl.pallas_call(
        functools.partial(reduce_kernel, tm_dims, region_dims, parts),
        out_shape=jax.ShapeDtypeStruct((2,) * len(region_dims) + (rows, nodes), BF16),
        in_specs=[vmem],
        out_specs=vmem,
        scratch_shapes=buffers + ends,
        compiler_params=pltpu.CompilerParams(
            collective_id=1, has_side_effects=True, vmem_limit_bytes=56 * 2**20
        ),
        name="reduce",
    )(grads)


def staged_parts(unit, layers, per, orders):
    by_x, by_y, by_z = orders
    third = per * unit // 3 // 16 * 16
    early = per * unit - 2 * third
    parts, stages = [], {}

    def add(stage, start, height, order):
        stages.setdefault(stage, []).append(len(parts))
        parts.append((start, height, order))

    add("output", 0, early - (early - third) // 2 // 16 * 16, by_x)
    second = parts[0][1]
    add("output", second, per * unit - second - third, by_y)
    add("output", per * unit - third, third, by_z)
    cycle = [by_z, by_x, by_y]
    for n, l in enumerate(reversed(range(layers))):
        add(l, (per + n) * unit, unit, cycle[n % 3])
    tail = (per + layers) * unit
    cut = unit // 2 // 16 * 16
    if cut:
        add("input", tail, cut, by_y)
    add("input", tail + cut, unit - cut, by_z)
    return parts, stages


def step_kernel(
    nt, tm_dims, region_dims, parts, stages,
    cov, obs, w_input, w_filter, w_mixing, w_output, cov_grad, out,
    scen, scored, v_input, v_filter, v_mixing, v_output, load_sem, grads, *refs,
):
    edges = Edges(nt, cov, obs, *refs[:6])
    halving = Halving(grads, tm_dims, region_dims, parts, refs[6:-3], *refs[-3:])
    barrier = pltpu.get_barrier_semaphore()
    edges.greet(barrier)
    for dim in region_dims:
        pl.semaphore_signal(barrier, inc=1, device_id=halving.across(dim), device_id_type=MESH)
    loads = {}
    pairs = (("input", w_input, v_input), ("filter", w_filter, v_filter),
             ("mixing", w_mixing, v_mixing), ("output", w_output, v_output))
    for n, (name, src, dst) in enumerate(pairs):
        loads[name] = pltpu.make_async_copy(src, dst, load_sem.at[n])
        loads[name].start()
    edges.own_squares()
    pl.semaphore_wait(barrier, nt - 1 + len(region_dims))
    edges.start()

    nodes = cov.shape[2]
    layers, channels = w_mixing.shape[:2]
    unit = channels // nt
    per = w_output.shape[1] // nodes // 4
    every = (slice(None),) * len(tm_dims)

    def need(name):
        if name == "cov":
            edges.arrived(0, 2)
        elif name == "obs":
            edges.arrived(2, 3)
        elif name == "total":
            edges.arrived(3, None)
            return edges.total()
        else:
            loads[name].wait()

    def put(owners, sub, at, value):
        free = sum(1 for o in owners if isinstance(o, slice))
        index = owners + (sub // 2, sub % 2, slice(at * unit, (at + 1) * unit), slice(None))
        grads[index] = value.reshape((2,) * free + (unit, nodes)).astype(BF16)

    def emit(name, index, part):
        if name == "output":
            put(every, index // per, index % per, part)
        elif name == "mixing":
            put(every, index, per + layers, part)
        elif name == "input":
            put(every, layers, per + layers, part)
        else:
            l, tap = index
            for h in range(2):
                piece = part[:, h * nodes : (h + 1) * nodes].reshape(nt // 2, 2, unit, nodes)
                for q in range(2):
                    put((tap,) + every[1:], h * 2 + q, per + layers - 1 - l, piece[:, q])

    def after(stage):
        if stage != "output":
            halving.round()
        for i in stages.get(stage, []):
            halving.begin(i)

    network(
        nt, cov, obs, *edges.got, v_input, v_filter, v_mixing, v_output, cov_grad, scen, scored,
        need, emit, after,
    )
    halving.finish()
    edges.sent()
    out[...] = halving.whole[...]


def run_step(nt, nr, cov, obs, weights):
    seqs, rows, nodes = cov.shape
    w_input, w_filter, w_mixing, w_output = weights
    layers, channels = w_mixing.shape[:2]
    unit = channels // nt
    per = w_output.shape[1] // nodes // nr
    tm_dims, region_dims = bit_dims(nt, nr)
    parts, stages = staged_parts(unit, layers, per, orders_of(tm_dims, region_dims))
    chunk = (per + layers + 1) * unit
    buffers, ends = halving_scratch(tm_dims, region_dims, parts, chunk, nodes)
    vmem, anywhere = pl.BlockSpec(memory_space=pltpu.VMEM), pl.BlockSpec(memory_space=pl.ANY)
    dims = len(tm_dims) + len(region_dims)
    return pl.pallas_call(
        functools.partial(step_kernel, nt, tm_dims, region_dims, parts, stages),
        out_shape=(
            jax.ShapeDtypeStruct(cov.shape, BF16),
            jax.ShapeDtypeStruct((2,) * len(region_dims) + (chunk, nodes), BF16),
        ),
        in_specs=[vmem] * 2 + [anywhere] * 4,
        out_specs=(vmem, vmem),
        scratch_shapes=network_scratch(cov, w_output)
        + [pltpu.VMEM(w.shape, BF16) for w in weights]
        + [
            pltpu.SemaphoreType.DMA((4,)),
            pltpu.VMEM((2,) * dims + (chunk, nodes), BF16),
            pltpu.VMEM((seqs, 16, nodes), BF16),
            pltpu.VMEM((seqs, 16, nodes), BF16),
            pltpu.VMEM((seqs, HALO, nodes), F32),
            pltpu.VMEM((nt, seqs, 8, 128), F32),
            pltpu.SemaphoreType.DMA((nt + 2,)),
            pltpu.SemaphoreType.DMA((nt + 2,)),
        ]
        + buffers
        + ends,
        compiler_params=pltpu.CompilerParams(
            collective_id=2, has_side_effects=True, vmem_limit_bytes=56 * 2**20
        ),
        name="step",
    )(cov, obs, *weights)


def unpack_kernel(cov_grad, whole, o_cov, o_input, o_filter, o_mixing, o_output):
    unit, nodes = o_input.shape
    layers = o_filter.shape[0]
    scenarios = o_output.shape[1] // nodes
    per = scenarios // 4

    def piece(sub, at):
        return whole[sub // 2, sub % 2, at * unit : (at + 1) * unit, :]

    o_cov[...] = cov_grad[...]
    for s in range(scenarios):
        o_output[:, s * nodes : (s + 1) * nodes] = piece(s // per, s % per)
    for l in range(layers):
        for h in range(2):
            for q in range(2):
                o_filter[l, q * unit : (q + 1) * unit, h * nodes : (h + 1) * nodes] = piece(
                    h * 2 + q, per + layers - 1 - l
                )
        o_mixing[l] = piece(l, per + layers)
    o_input[...] = piece(layers, per + layers)


def unpack(cov_grad, summed, shapes):
    vmem = pl.BlockSpec(memory_space=pltpu.VMEM)
    shapes = (cov_grad.shape,) + shapes
    return pl.pallas_call(
        unpack_kernel,
        out_shape=tuple(jax.ShapeDtypeStruct(s, BF16) for s in shapes),
        in_specs=[vmem] * 2,
        out_specs=(vmem,) * len(shapes),
        name="unpack",
    )(cov_grad, summed)


def per_device(nt, nr, cov, obs, w_input, w_filter, w_mixing, w_output):
    nodes = cov.shape[2]
    weights = (w_input, w_filter, w_mixing, w_output)
    layers, channels = w_mixing.shape[:2]
    scenarios = w_output.shape[1] // nodes
    unit = channels // nt
    shapes = (
        (unit, nodes), (layers, 2 * unit, 2 * channels), (layers, unit, channels), (unit, scenarios * nodes)
    )
    if unit % 16 == 0 and nr == 4 and layers == 3 and scenarios % 4 == 0 and channels == nodes:
        return tuple(unpack(*run_step(nt, nr, cov, obs, weights), shapes))
    edges = exchange_edges(nt, cov, obs)
    cov_grad, *grads = run_network(nt, cov, obs, edges, weights)
    sources = tuple(
        jnp.moveaxis(g.reshape(g.shape[:-2] + (nt, -1) + g.shape[-1:]), -3, 0) for g in grads
    )
    flat = jnp.concatenate([s.reshape(nt, -1) for s in sources], axis=1).reshape(nt, -1, nodes)
    summed = reduce_grads(nt, nr, flat).reshape(-1)
    outs, first = [], 0
    for source, shape in zip(sources, shapes):
        size = source.size // nt
        outs.append(summed[first : first + size].reshape(shape))
        first += size
    return (cov_grad, *outs)


def solution(mesh):
    placed = (P("region", "tm", None), P("region", "tm", None), P(), P(), P(), P())
    return jax.shard_map(
        functools.partial(per_device, mesh.shape["tm"], mesh.shape["region"]),
        mesh=mesh,
        in_specs=placed,
        out_specs=(
            P("region", "tm", None),
            P("tm", None),
            P(None, "tm", None),
            P(None, "tm", None),
            P("tm", None),
        ),
        check_vma=False,
    )
```

```python
import functools

import jax
import jax.numpy as jnp
from jax import lax
from jax.experimental import pallas as pl
from jax.experimental.pallas import tpu as pltpu
from jax.sharding import PartitionSpec as P

MESH = pl.DeviceIdType.MESH
epsilon = 1e-05
HALO = 8
F32 = jnp.float32
BF16 = jnp.bfloat16


def dot(a, b, ca=1, cb=0, precision=None):
    return lax.dot_general(
        a, b, (((ca,), (cb,)), ((), ())), precision=precision, preferred_element_type=F32
    )


class Edges:
    def __init__(self, nt, cov, obs, got_prev, got_next, got_obs, sums, send_sem, recv_sem):
        self.nt, self.cov, self.obs, self.sums = nt, cov, obs, sums
        self.got = (got_prev, got_next, got_obs)
        self.send_sem, self.recv_sem = send_sem, recv_sem
        self.copies = []

    def at(self, offset):
        return {"tm": lax.rem(lax.axis_index("tm") + offset, self.nt)}

    def greet(self, barrier):
        for offset in range(1, self.nt):
            pl.semaphore_signal(barrier, inc=1, device_id=self.at(offset), device_id_type=MESH)

    def own_squares(self):
        seqs, rows, nodes = self.obs.shape
        sq = self.obs[...] * self.obs[...]
        sq = jnp.sum(sq.reshape(seqs, rows // 8, 8, nodes), axis=1)
        own = sq[:, :, :128]
        for part in range(1, nodes // 128):
            own = own + sq[:, :, part * 128 : (part + 1) * 128]
        self.sums[0] = own

    def send(self, src, dst, offset):
        slot = len(self.copies)
        copy = pltpu.make_async_remote_copy(
            src_ref=src, dst_ref=dst,
            send_sem=self.send_sem.at[slot], recv_sem=self.recv_sem.at[slot],
            device_id=self.at(offset), device_id_type=MESH,
        )
        copy.start()
        self.copies.append(copy)

    def start(self):
        nt, rows = self.nt, self.cov.shape[1]
        self.send(self.cov.at[:, pl.ds(rows - 16, 16), :], self.got[0], 1)
        self.send(self.cov.at[:, pl.ds(0, 16), :], self.got[1], nt - 1)
        self.send(self.obs.at[:, pl.ds(0, HALO), :], self.got[2], nt - 1)
        for offset in range(1, nt):
            self.send(self.sums.at[0], self.sums.at[offset], offset)

    def arrived(self, first, last):
        for copy in self.copies[first:last]:
            copy.wait_recv()

    def sent(self):
        for copy in self.copies:
            copy.wait_send()

    def total(self):
        return jnp.sum(self.sums[...], axis=0)


def edges_kernel(nt, cov, obs, prev_cov, next_cov, next_obs, total, *scratch):
    edges = Edges(nt, cov, obs, *scratch)
    barrier = pltpu.get_barrier_semaphore()
    edges.greet(barrier)
    edges.own_squares()
    pl.semaphore_wait(barrier, nt - 1)
    edges.start()
    edges.arrived(0, None)
    edges.sent()
    for out, got in zip((prev_cov, next_cov, next_obs), edges.got):
        out[...] = got[...]
    total[...] = edges.total()


def exchange_edges(nt, cov, obs):
    seqs, rows, nodes = cov.shape
    vmem = pl.BlockSpec(memory_space=pltpu.VMEM)
    edge = jax.ShapeDtypeStruct((seqs, 16, nodes), BF16)
    copies = nt + 2
    return pl.pallas_call(
        functools.partial(edges_kernel, nt),
        out_shape=(
            edge,
            edge,
            jax.ShapeDtypeStruct((seqs, HALO, nodes), F32),
            jax.ShapeDtypeStruct((seqs, 8, 128), F32),
        ),
        in_specs=[vmem] * 2,
        out_specs=(vmem,) * 4,
        scratch_shapes=[
            pltpu.VMEM((seqs, 16, nodes), BF16),
            pltpu.VMEM((seqs, 16, nodes), BF16),
            pltpu.VMEM((seqs, HALO, nodes), F32),
            pltpu.VMEM((nt, seqs, 8, 128), F32),
            pltpu.SemaphoreType.DMA((copies,)),
            pltpu.SemaphoreType.DMA((copies,)),
        ],
        compiler_params=pltpu.CompilerParams(collective_id=0, has_side_effects=True),
        name="edges",
    )(cov, obs)


def network(
    nt, cov, obs, prev_cov, next_cov, next_obs, w_input, w_filter, w_mixing, w_output,
    cov_grad, scen, scored, need, emit, after,
):
    me = lax.axis_index("tm")
    seqs, rows, nodes = cov.shape
    layers = w_filter.shape[0]
    channels = w_mixing.shape[1]
    scenarios = w_output.shape[1] // nodes
    span = rows + 2 * HALO
    kept = rows + HALO
    halves = nodes // 128
    not_first = (me > 0).astype(F32)
    not_last = (me < nt - 1).astype(F32)

    def own_rows(x):
        return jnp.concatenate([x[b * span + HALO : b * span + HALO + rows] for b in range(seqs)], axis=0)

    cov_own = cov[...]
    need("cov")
    need("input")
    spans = []
    for b in range(seqs):
        spans.append(prev_cov[b].astype(F32)[16 - HALO :] * not_first)
        spans.append(cov_own[b].astype(F32))
        spans.append(next_cov[b].astype(F32)[:HALO])
    hidden = dot(jnp.concatenate(spans, axis=0).astype(BF16), w_input[...]).astype(BF16).astype(F32)
    stored = []
    need("filter")
    need("mixing")
    for l in range(layers):
        delayed = pltpu.roll(hidden, 2**l, 0)
        joined = jnp.concatenate([delayed, hidden], axis=1).astype(BF16)
        preact = dot(joined, w_filter[l])
        act = jnp.tanh(preact[:, :channels])
        gate = 0.5 * jnp.tanh(0.5 * preact[:, channels:]) + 0.5
        gated = (act * gate).astype(BF16)
        stored.append((delayed, hidden, act, gate))
        hidden = (hidden + dot(gated, w_mixing[l])).astype(BF16).astype(F32)

    last = jnp.concatenate([hidden[b * span + HALO : (b + 1) * span] for b in range(seqs)], axis=0)
    last = last.astype(BF16)
    need("output")
    batch = 4 if scenarios % 4 == 0 else 1

    def columns(s):
        return pl.ds(pl.multiple_of(s * nodes, nodes), nodes)

    def predict(j, carry):
        for k in range(batch):
            s = j * batch + k
            pred = dot(last, w_output[:, columns(s)])
            for h in range(halves):
                scen[h, pl.ds(s, seqs * kept, stride=scenarios), :] = pred[:, h * 128 : (h + 1) * 128]
        return carry

    lax.fori_loop(0, scenarios // batch, predict, 0)
    need("obs")
    for b in range(seqs):
        scored[b * kept : b * kept + rows] = obs[b]
        scored[b * kept + rows : (b + 1) * kept] = next_obs[b]

    block = 16 * scenarios
    row_no = lax.broadcasted_iota(jnp.int32, (block, block), 0)
    col_no = lax.broadcasted_iota(jnp.int32, (block, block), 1)
    same_step = (row_no // scenarios) == (col_no // scenarios)
    diagonal = row_no == col_no
    pairs = jnp.where(same_step & ~diagonal, 1.0 / (scenarios * (scenarios - 1) * nodes), 0.0)

    def score(groups):
        ats = [pl.ds(pl.multiple_of(g * block, block), block) for g in groups]
        ys = [jnp.concatenate([scen[h, at, :] for h in range(halves)], axis=1) for at in ats]
        highs = [y.astype(BF16) for y in ys]
        lows = [(y - hi.astype(F32)).astype(BF16) for y, hi in zip(ys, highs)]
        grams = [
            dot(jnp.concatenate([hi, lo, hi, lo], axis=1), jnp.concatenate([hi, hi, lo, lo], axis=1), 1, 1)
            for hi, lo in zip(highs, lows)
        ]
        targets = []
        for g, y in zip(groups, ys):
            o = scored[pl.ds(pl.multiple_of(g * 16, 16), 16), :]
            diff = y - jnp.broadcast_to(o[:, None, :], (16, scenarios, nodes)).reshape(block, nodes)
            inv = lax.rsqrt(jnp.sum(diff * diff, axis=1, keepdims=True) * (1.0 / nodes) + epsilon)
            targets.append(inv * (1.0 / (scenarios * nodes)) * diff)
        coefs = []
        for gram in grams:
            own = jnp.where(diagonal, gram, 0.0)
            own_sq = jnp.sum(own, axis=1, keepdims=True) + jnp.sum(own, axis=0, keepdims=True)
            pair_sq = jnp.maximum(own_sq - 2.0 * gram, 0.0) * (1.0 / nodes)
            coefs.append(pairs * lax.rsqrt(pair_sq + epsilon))
        for at, y, hi, lo, coef, target in zip(ats, ys, highs, lows, coefs, targets):
            chi = coef.astype(BF16)
            clo = (coef - chi.astype(F32)).astype(BF16)
            mixed = dot(jnp.concatenate([chi, clo, chi], axis=1), jnp.concatenate([hi, hi, lo], axis=0))
            grad = mixed - jnp.sum(coef, axis=1, keepdims=True) * y + target
            for h in range(halves):
                scen[h, at, :] = grad[:, h * 128 : (h + 1) * 128]

    groups = seqs * kept // 16

    def score_pair(i, carry):
        score([2 * i, 2 * i + 1])
        return carry

    lax.fori_loop(0, groups // 2, score_pair, 0)
    if groups % 2:
        score([groups - 1])

    length = rows * nt
    step_no = lax.broadcasted_iota(jnp.int32, (kept, 1), 0)
    valid = jnp.where(step_no < rows, 1.0, not_last)
    factor = []
    total = need("total")
    for b in range(seqs):
        sq = jnp.sum(jnp.sum(total[b], axis=1, keepdims=True), axis=0, keepdims=True)
        factor.append(valid * lax.rsqrt(sq / (length * nodes) + epsilon))
    factor = jnp.concatenate(factor, axis=0)

    def kept_own(x):
        return jnp.concatenate([x[b * kept : b * kept + rows] for b in range(seqs)], axis=0)

    last_own = own_rows(hidden).T.astype(BF16)

    def output_step(j, grad_last):
        for k in range(batch):
            s = j * batch + k
            g = jnp.concatenate(
                [scen[h, pl.ds(s, seqs * kept, stride=scenarios), :] for h in range(halves)], axis=1
            )
            g = g * factor
            grad_last = grad_last + dot(g.astype(BF16), w_output[:, columns(s)], 1, 1)
            emit("output", (j, k), dot(last_own, kept_own(g).astype(BF16)))
        return grad_last

    grad_last = jnp.zeros((seqs * kept, channels), F32)
    grad_last = lax.fori_loop(0, scenarios // batch, output_step, grad_last)
    after("output")
    grad_last = grad_last.astype(BF16).astype(F32)
    pieces = []
    for b in range(seqs):
        pieces.append(jnp.zeros((HALO, channels), F32))
        pieces.append(grad_last[b * kept : (b + 1) * kept])
    grad = jnp.concatenate(pieces, axis=0)

    for l in reversed(range(layers)):
        delayed, held, act, gate = stored[l]
        grad16 = grad.astype(BF16)
        gated_t = own_rows(act * gate).T.astype(BF16)
        part = dot(gated_t, own_rows(grad).astype(BF16))
        emit("mixing", l, part)
        gated_cot = dot(grad16, w_mixing[l], 1, 1).astype(BF16).astype(F32)
        pre = jnp.concatenate(
            [gated_cot * gate * (1.0 - act * act), gated_cot * act * gate * (1.0 - gate)], axis=1
        )
        own_pre = own_rows(pre).astype(BF16)
        for tap, source in enumerate((delayed, held)):
            part = dot(own_rows(source).T.astype(BF16), own_pre)
            emit("filter", (l, tap), part)
        after(l)
        both = dot(pre.astype(BF16), w_filter[l], 1, 1).astype(BF16).astype(F32)
        past = pltpu.roll(both[:, :channels], seqs * span - 2**l, 0)
        grad = (grad + both[:, channels:] + past).astype(BF16).astype(F32)

    own = own_rows(grad).astype(BF16)
    cov_flat = jnp.concatenate([cov_own[b] for b in range(seqs)], axis=0)
    part = dot(cov_flat.astype(F32).T.astype(BF16), own)
    emit("input", None, part)
    after("input")
    result = dot(own, w_input[...], 1, 1).astype(BF16)
    for b in range(seqs):
        cov_grad[b] = result[b * rows : (b + 1) * rows]


def network_kernel(nt, cov, obs, prev_cov, next_cov, next_obs, total, *rest):
    weights, cov_grad, grads, (scen, scored) = rest[:4], rest[4], rest[5:9], rest[9:]
    g_input, g_filter, g_mixing, g_output = grads
    nodes, channels = cov.shape[2], weights[2].shape[1]

    def need(name):
        return total[...] if name == "total" else None

    def emit(name, index, part):
        part = part.astype(BF16)
        if name == "output":
            j, k = index
            batch = 4 if g_output.shape[1] // nodes % 4 == 0 else 1
            g_output[:, pl.ds(pl.multiple_of((j * batch + k) * nodes, nodes), nodes)] = part
        elif name == "mixing":
            g_mixing[index] = part
        elif name == "filter":
            l, tap = index
            g_filter[l, tap * channels : (tap + 1) * channels, :] = part
        else:
            g_input[...] = part

    network(
        nt, cov, obs, prev_cov, next_cov, next_obs, *weights, cov_grad, scen, scored,
        need, emit, lambda stage: None,
    )


def network_scratch(cov, w_output):
    seqs, rows, nodes = cov.shape
    steps = seqs * (rows + HALO)
    scenarios = w_output.shape[1] // nodes
    return [
        pltpu.VMEM((nodes // 128, steps * scenarios, 128), F32),
        pltpu.VMEM((steps, nodes), F32),
    ]


def run_network(nt, cov, obs, edges, weights):
    vmem = pl.BlockSpec(memory_space=pltpu.VMEM)
    grads = tuple(jax.ShapeDtypeStruct(w.shape, BF16) for w in weights)
    return pl.pallas_call(
        functools.partial(network_kernel, nt),
        out_shape=(jax.ShapeDtypeStruct(cov.shape, BF16),) + grads,
        in_specs=[vmem] * 10,
        out_specs=(vmem,) * (1 + len(grads)),
        scratch_shapes=network_scratch(cov, weights[3]),
        compiler_params=pltpu.CompilerParams(vmem_limit_bytes=56 * 2**20),
        name="network",
    )(cov, obs, *edges, *weights)


def bit_dims(nt, nr):
    bits = lambda n: n.bit_length() - 1
    tm_dims = [("tm", 2**i) for i in reversed(range(bits(nt)))]
    region_dims = [("region", 2**i) for i in reversed(range(bits(nr)))]
    return tm_dims, region_dims


def orders_of(tm_dims, region_dims):
    near = region_dims[-1:]
    x, ys = region_dims[:-1], list(reversed(tm_dims))
    y, z = ys[:1], ys[1:]
    return [near + x + y + z, near + y + z[:1] + x + z[1:], near + z[:1] + x + y + z[1:]]


def even_parts(rows, orders):
    units = rows // 16
    count = min(2 * len(orders), units)
    cuts = [16 * (units * i // count) for i in range(count + 1)]
    return [(cuts[i], cuts[i + 1] - cuts[i], orders[i % 3]) for i in range(count)]


class Halving:
    def __init__(self, sources, tm_dims, region_dims, parts, buffers, whole, send_sem, recv_sem):
        self.dims, self.region_dims, self.parts = tm_dims + region_dims, region_dims, parts
        self.whole = whole
        self.send_sem, self.recv_sem = send_sem, recv_sem
        n = len(self.dims)
        self.buffers = [buffers[i * n : (i + 1) * n] for i in range(len(parts))]
        self.current = list(sources)
        self.phase = [0 for _ in parts]
        self.flying = [None for _ in parts]
        self.done = []
        self.slot = 0
        self.where = {"tm": lax.axis_index("tm"), "region": lax.axis_index("region")}

    def bit(self, dim):
        axis, weight = dim
        return lax.rem(lax.div(self.where[axis], weight), 2)

    def across(self, dim):
        axis, weight = dim
        return {axis: self.where[axis] + weight * (1 - 2 * self.bit(dim))}

    def copy(self, i, src, dst, dim):
        copy = pltpu.make_async_remote_copy(
            src_ref=src, dst_ref=dst,
            send_sem=self.send_sem.at[self.slot], recv_sem=self.recv_sem.at[self.slot],
            device_id=self.across(dim), device_id_type=MESH,
        )
        self.slot += 1
        copy.start()
        self.flying[i] = copy

    def rows_at(self, i):
        return pl.ds(self.parts[i][0], self.parts[i][1])

    def send_half(self, i):
        dim = self.parts[i][2][self.phase[i]]
        self.copy(i, self.current[i].at[1 - self.bit(dim)], self.buffers[i][self.phase[i]], dim)

    def send_whole(self, i, n):
        index = tuple(slice(None) if m < n else self.bit(d) for m, d in enumerate(self.region_dims))
        index = index + (self.rows_at(i), slice(None))
        self.copy(i, self.whole.at[index], self.whole.at[index], self.region_dims[n])

    def begin(self, i):
        self.send_half(i)

    def advance(self, i):
        if self.flying[i] is None:
            return False
        self.flying[i].wait_recv()
        self.done.append(self.flying[i])
        self.flying[i] = None
        phase, last = self.phase[i], len(self.dims)
        if phase < last:
            dim = self.parts[i][2][phase]
            into = self.buffers[i][phase]
            mine = self.current[i][self.bit(dim)]
            into[...] = (into[...].astype(F32) + mine.astype(F32)).astype(BF16)
            self.current[i] = into
            self.phase[i] += 1
            if phase + 1 < last:
                self.send_half(i)
            else:
                index = tuple(self.bit(d) for d in self.region_dims)
                self.whole[index + (self.rows_at(i), slice(None))] = into[...]
                self.send_whole(i, 0)
        else:
            self.phase[i] += 1
            if phase + 1 - last < len(self.region_dims):
                self.send_whole(i, phase + 1 - last)
        return True

    def round(self):
        return any([self.advance(i) for i in range(len(self.parts))])

    def finish(self):
        while self.round():
            pass
        for copy in self.done:
            copy.wait_send()


def halving_scratch(tm_dims, region_dims, parts, rows, nodes):
    n = len(tm_dims) + len(region_dims)
    scratch = []
    for _, height, _ in parts:
        for phase in range(n):
            scratch.append(pltpu.VMEM((2,) * (n - phase - 1) + (height, nodes), BF16))
    copies = len(parts) * (n + len(region_dims))
    return scratch, [
        pltpu.VMEM((2,) * len(region_dims) + (rows, nodes), BF16),
        pltpu.SemaphoreType.DMA((copies,)),
        pltpu.SemaphoreType.DMA((copies,)),
    ]


def reduce_kernel(tm_dims, region_dims, parts, *refs):
    sources, out, refs = refs[: len(parts)], refs[len(parts)], refs[len(parts) + 1 :]
    halving = Halving(sources, tm_dims, region_dims, parts, refs[:-3], *refs[-3:])
    barrier = pltpu.get_barrier_semaphore()
    for dim in halving.dims:
        pl.semaphore_signal(barrier, inc=1, device_id=halving.across(dim), device_id_type=MESH)
    pl.semaphore_wait(barrier, len(halving.dims))
    for i in range(len(parts)):
        halving.begin(i)
    halving.finish()
    out[...] = halving.whole[...]


def reduce_grads(nt, nr, grads):
    _, width, nodes = grads.shape
    rows = width // nr
    tm_dims, region_dims = bit_dims(nt, nr)
    parts = even_parts(rows, orders_of(tm_dims, region_dims))
    grads = grads.reshape((2,) * (len(tm_dims) + len(region_dims)) + (rows, nodes))
    dims = tm_dims + region_dims
    sources = []
    for start, height, order in parts:
        moved = tuple(dims.index(d) for d in order) + (len(dims), len(dims) + 1)
        sources.append(jnp.transpose(grads[..., start : start + height, :], moved))
    buffers, ends = halving_scratch(tm_dims, region_dims, parts, rows, nodes)
    vmem = pl.BlockSpec(memory_space=pltpu.VMEM)
    return pl.pallas_call(
        functools.partial(reduce_kernel, tm_dims, region_dims, parts),
        out_shape=jax.ShapeDtypeStruct((2,) * len(region_dims) + (rows, nodes), BF16),
        in_specs=[vmem] * len(sources),
        out_specs=vmem,
        scratch_shapes=buffers + ends,
        compiler_params=pltpu.CompilerParams(
            collective_id=1, has_side_effects=True, vmem_limit_bytes=56 * 2**20
        ),
        name="reduce",
    )(*sources)


def staged_parts(unit, layers, per, orders):
    by_x, by_y, by_z = orders
    third = per * unit // 3 // 16 * 16
    early = per * unit - 2 * third
    parts, stages = [], {}

    def add(stage, start, height, order):
        stages.setdefault(stage, []).append(len(parts))
        parts.append((start, height, order))

    add("output", 0, early - (early - third) // 2 // 16 * 16, by_x)
    second = parts[0][1]
    add("output", second, per * unit - second - third, by_y)
    add("output", per * unit - third, third, by_z)
    early_layers = (layers + 1) // 2
    add(layers - early_layers, per * unit, early_layers * unit, by_z)
    tail = (per + early_layers) * unit
    rest = (layers + 1 - early_layers) * unit
    cut = rest // 2 // 16 * 16
    add("input", tail, cut, by_x)
    add("input", tail + cut, rest - cut, by_y)
    return parts, stages


def step_kernel(
    nt, tm_dims, region_dims, parts, stages,
    cov, obs, w_input, w_filter, w_mixing, w_output, cov_grad, out,
    scen, scored, v_input, v_filter, v_mixing, v_output, load_sem, *refs,
):
    edges = Edges(nt, cov, obs, *refs[:6])
    sources, refs = refs[6 : 6 + len(parts)], refs[len(parts) :]
    halving = Halving(sources, tm_dims, region_dims, parts, refs[6:-3], *refs[-3:])
    barrier = pltpu.get_barrier_semaphore()
    edges.greet(barrier)
    for dim in region_dims:
        pl.semaphore_signal(barrier, inc=1, device_id=halving.across(dim), device_id_type=MESH)
    loads = {}
    pairs = (("input", w_input, v_input), ("filter", w_filter, v_filter),
             ("mixing", w_mixing, v_mixing), ("output", w_output, v_output))
    for n, (name, src, dst) in enumerate(pairs):
        loads[name] = pltpu.make_async_copy(src, dst, load_sem.at[n])
        loads[name].start()
    edges.own_squares()
    pl.semaphore_wait(barrier, nt - 1 + len(region_dims))
    edges.start()

    nodes = cov.shape[2]
    layers, channels = w_mixing.shape[:2]
    unit = channels // nt
    per = w_output.shape[1] // nodes // 4
    every = range(nt)

    def need(name):
        if name == "cov":
            edges.arrived(0, 2)
        elif name == "obs":
            edges.arrived(2, 3)
        elif name == "total":
            edges.arrived(3, None)
            return edges.total()
        else:
            loads[name].wait()

    def put(owners, sub, at, value):
        value = value.reshape(len(owners), unit, nodes).astype(BF16)
        place = {("region", 2): lax.div(sub, 2), ("region", 1): lax.rem(sub, 2)}
        for source, (start, height, order) in zip(sources, parts):
            low, high = max(start, at * unit), min(start + height, (at + 1) * unit)
            if low >= high:
                continue
            for j, owner in enumerate(owners):
                index = tuple(place[d] if d in place else owner // d[1] % 2 for d in order)
                index = index + (slice(low - start, high - start), slice(None))
                source[index] = value[j, low - at * unit : high - at * unit]

    def emit(name, index, part):
        if name == "output":
            put(every, index[0], index[1], part)
        elif name == "mixing":
            put(every, index, per + layers, part)
        elif name == "input":
            put(every, layers, per + layers, part)
        else:
            l, tap = index
            owners = range(tap * nt // 2, (tap + 1) * nt // 2)
            for h in range(2):
                piece = part[:, h * nodes : (h + 1) * nodes].reshape(nt // 2, 2, unit, nodes)
                for q in range(2):
                    put(owners, h * 2 + q, per + layers - 1 - l, piece[:, q])

    def after(stage):
        if stage not in ("output", layers - 1):
            halving.round()
        for i in stages.get(stage, []):
            halving.begin(i)

    network(
        nt, cov, obs, *edges.got, v_input, v_filter, v_mixing, v_output, cov_grad, scen, scored,
        need, emit, after,
    )
    halving.finish()
    edges.sent()
    out[...] = halving.whole[...]


def run_step(nt, nr, cov, obs, weights):
    seqs, rows, nodes = cov.shape
    w_input, w_filter, w_mixing, w_output = weights
    layers, channels = w_mixing.shape[:2]
    unit = channels // nt
    per = w_output.shape[1] // nodes // nr
    tm_dims, region_dims = bit_dims(nt, nr)
    parts, stages = staged_parts(unit, layers, per, orders_of(tm_dims, region_dims))
    chunk = (per + layers + 1) * unit
    buffers, ends = halving_scratch(tm_dims, region_dims, parts, chunk, nodes)
    vmem, anywhere = pl.BlockSpec(memory_space=pltpu.VMEM), pl.BlockSpec(memory_space=pl.ANY)
    dims = len(tm_dims) + len(region_dims)
    return pl.pallas_call(
        functools.partial(step_kernel, nt, tm_dims, region_dims, parts, stages),
        out_shape=(
            jax.ShapeDtypeStruct(cov.shape, BF16),
            jax.ShapeDtypeStruct((2,) * len(region_dims) + (chunk, nodes), BF16),
        ),
        in_specs=[vmem] * 2 + [anywhere] * 4,
        out_specs=(vmem, vmem),
        scratch_shapes=network_scratch(cov, w_output)
        + [pltpu.VMEM(w.shape, BF16) for w in weights]
        + [
            pltpu.SemaphoreType.DMA((4,)),
            pltpu.VMEM((seqs, 16, nodes), BF16),
            pltpu.VMEM((seqs, 16, nodes), BF16),
            pltpu.VMEM((seqs, HALO, nodes), F32),
            pltpu.VMEM((nt, seqs, 8, 128), F32),
            pltpu.SemaphoreType.DMA((nt + 2,)),
            pltpu.SemaphoreType.DMA((nt + 2,)),
        ]
        + [pltpu.VMEM((2,) * dims + (height, nodes), BF16) for _, height, _ in parts]
        + buffers
        + ends,
        compiler_params=pltpu.CompilerParams(
            collective_id=2, has_side_effects=True, vmem_limit_bytes=56 * 2**20
        ),
        name="step",
    )(cov, obs, *weights)


def unpack_kernel(cov_grad, whole, o_cov, o_input, o_filter, o_mixing, o_output):
    unit, nodes = o_input.shape
    layers = o_filter.shape[0]
    scenarios = o_output.shape[1] // nodes
    per = scenarios // 4

    def piece(sub, at):
        return whole[sub // 2, sub % 2, at * unit : (at + 1) * unit, :]

    o_cov[...] = cov_grad[...]
    for s in range(scenarios):
        o_output[:, s * nodes : (s + 1) * nodes] = piece(s // per, s % per)
    for l in range(layers):
        for h in range(2):
            for q in range(2):
                o_filter[l, q * unit : (q + 1) * unit, h * nodes : (h + 1) * nodes] = piece(
                    h * 2 + q, per + layers - 1 - l
                )
        o_mixing[l] = piece(l, per + layers)
    o_input[...] = piece(layers, per + layers)


def unpack(cov_grad, summed, shapes):
    vmem = pl.BlockSpec(memory_space=pltpu.VMEM)
    shapes = (cov_grad.shape,) + shapes
    return pl.pallas_call(
        unpack_kernel,
        out_shape=tuple(jax.ShapeDtypeStruct(s, BF16) for s in shapes),
        in_specs=[vmem] * 2,
        out_specs=(vmem,) * len(shapes),
        name="unpack",
    )(cov_grad, summed)


def per_device(nt, nr, cov, obs, w_input, w_filter, w_mixing, w_output):
    nodes = cov.shape[2]
    weights = (w_input, w_filter, w_mixing, w_output)
    layers, channels = w_mixing.shape[:2]
    scenarios = w_output.shape[1] // nodes
    unit = channels // nt
    shapes = (
        (unit, nodes), (layers, 2 * unit, 2 * channels), (layers, unit, channels), (unit, scenarios * nodes)
    )
    if unit % 16 == 0 and nr == 4 and layers == 3 and scenarios == 16 and channels == nodes:
        return tuple(unpack(*run_step(nt, nr, cov, obs, weights), shapes))
    edges = exchange_edges(nt, cov, obs)
    cov_grad, *grads = run_network(nt, cov, obs, edges, weights)
    sources = tuple(
        jnp.moveaxis(g.reshape(g.shape[:-2] + (nt, -1) + g.shape[-1:]), -3, 0) for g in grads
    )
    flat = jnp.concatenate([s.reshape(nt, -1) for s in sources], axis=1).reshape(nt, -1, nodes)
    summed = reduce_grads(nt, nr, flat).reshape(-1)
    outs, first = [], 0
    for source, shape in zip(sources, shapes):
        size = source.size // nt
        outs.append(summed[first : first + size].reshape(shape))
        first += size
    return (cov_grad, *outs)


def solution(mesh):
    placed = (P("region", "tm", None), P("region", "tm", None), P(), P(), P(), P())
    return jax.shard_map(
        functools.partial(per_device, mesh.shape["tm"], mesh.shape["region"]),
        mesh=mesh,
        in_specs=placed,
        out_specs=(
            P("region", "tm", None),
            P("tm", None),
            P(None, "tm", None),
            P(None, "tm", None),
            P("tm", None),
        ),
        check_vma=False,
    )
```

```python
import functools

import jax
import jax.numpy as jnp
from jax import lax
from jax.experimental import pallas as pl
from jax.experimental.pallas import tpu as pltpu
from jax.sharding import PartitionSpec as P

MESH = pl.DeviceIdType.MESH
epsilon = 1e-05
HALO = 8
F32 = jnp.float32
BF16 = jnp.bfloat16


def dot(a, b, ca=1, cb=0, precision=None):
    return lax.dot_general(
        a, b, (((ca,), (cb,)), ((), ())), precision=precision, preferred_element_type=F32
    )


class Edges:
    def __init__(self, nt, cov, obs, got_prev, got_next, got_obs, sums, send_sem, recv_sem):
        self.nt, self.cov, self.obs, self.sums = nt, cov, obs, sums
        self.got = (got_prev, got_next, got_obs)
        self.send_sem, self.recv_sem = send_sem, recv_sem
        self.copies = []

    def at(self, offset):
        return {"tm": lax.rem(lax.axis_index("tm") + offset, self.nt)}

    def greet(self, barrier):
        for offset in range(1, self.nt):
            pl.semaphore_signal(barrier, inc=1, device_id=self.at(offset), device_id_type=MESH)

    def own_squares(self):
        seqs, rows, nodes = self.obs.shape
        sq = self.obs[...] * self.obs[...]
        sq = jnp.sum(sq.reshape(seqs, rows // 8, 8, nodes), axis=1)
        own = sq[:, :, :128]
        for part in range(1, nodes // 128):
            own = own + sq[:, :, part * 128 : (part + 1) * 128]
        self.sums[0] = own

    def send(self, src, dst, offset):
        slot = len(self.copies)
        copy = pltpu.make_async_remote_copy(
            src_ref=src, dst_ref=dst,
            send_sem=self.send_sem.at[slot], recv_sem=self.recv_sem.at[slot],
            device_id=self.at(offset), device_id_type=MESH,
        )
        copy.start()
        self.copies.append(copy)

    def start(self):
        nt, rows = self.nt, self.cov.shape[1]
        self.send(self.cov.at[:, pl.ds(rows - 16, 16), :], self.got[0], 1)
        self.send(self.cov.at[:, pl.ds(0, 16), :], self.got[1], nt - 1)
        self.send(self.obs.at[:, pl.ds(0, HALO), :], self.got[2], nt - 1)
        for offset in range(1, nt):
            self.send(self.sums.at[0], self.sums.at[offset], offset)

    def arrived(self, first, last):
        for copy in self.copies[first:last]:
            copy.wait_recv()

    def sent(self):
        for copy in self.copies:
            copy.wait_send()

    def total(self):
        return jnp.sum(self.sums[...], axis=0)


def edges_kernel(nt, cov, obs, prev_cov, next_cov, next_obs, total, *scratch):
    edges = Edges(nt, cov, obs, *scratch)
    barrier = pltpu.get_barrier_semaphore()
    edges.greet(barrier)
    edges.own_squares()
    pl.semaphore_wait(barrier, nt - 1)
    edges.start()
    edges.arrived(0, None)
    edges.sent()
    for out, got in zip((prev_cov, next_cov, next_obs), edges.got):
        out[...] = got[...]
    total[...] = edges.total()


def exchange_edges(nt, cov, obs):
    seqs, rows, nodes = cov.shape
    vmem = pl.BlockSpec(memory_space=pltpu.VMEM)
    edge = jax.ShapeDtypeStruct((seqs, 16, nodes), BF16)
    copies = nt + 2
    return pl.pallas_call(
        functools.partial(edges_kernel, nt),
        out_shape=(
            edge,
            edge,
            jax.ShapeDtypeStruct((seqs, HALO, nodes), F32),
            jax.ShapeDtypeStruct((seqs, 8, 128), F32),
        ),
        in_specs=[vmem] * 2,
        out_specs=(vmem,) * 4,
        scratch_shapes=[
            pltpu.VMEM((seqs, 16, nodes), BF16),
            pltpu.VMEM((seqs, 16, nodes), BF16),
            pltpu.VMEM((seqs, HALO, nodes), F32),
            pltpu.VMEM((nt, seqs, 8, 128), F32),
            pltpu.SemaphoreType.DMA((copies,)),
            pltpu.SemaphoreType.DMA((copies,)),
        ],
        compiler_params=pltpu.CompilerParams(collective_id=0, has_side_effects=True),
        name="edges",
    )(cov, obs)


def network(
    nt, cov, obs, prev_cov, next_cov, next_obs, w_input, w_filter, w_mixing, w_output,
    cov_grad, scen, scored, need, emit, after,
):
    me = lax.axis_index("tm")
    seqs, rows, nodes = cov.shape
    layers = w_filter.shape[0]
    channels = w_mixing.shape[1]
    scenarios = w_output.shape[1] // nodes
    span = rows + 2 * HALO
    kept = rows + HALO
    halves = nodes // 128
    not_first = (me > 0).astype(F32)
    not_last = (me < nt - 1).astype(F32)

    def own_rows(x):
        return jnp.concatenate([x[b * span + HALO : b * span + HALO + rows] for b in range(seqs)], axis=0)

    cov_own = cov[...]
    need("cov")
    need("input")
    spans = []
    for b in range(seqs):
        spans.append(prev_cov[b].astype(F32)[16 - HALO :] * not_first)
        spans.append(cov_own[b].astype(F32))
        spans.append(next_cov[b].astype(F32)[:HALO])
    hidden = dot(jnp.concatenate(spans, axis=0).astype(BF16), w_input[...]).astype(BF16).astype(F32)
    stored = []
    need("filter")
    need("mixing")
    for l in range(layers):
        delayed = pltpu.roll(hidden, 2**l, 0)
        joined = jnp.concatenate([delayed, hidden], axis=1).astype(BF16)
        preact = dot(joined, w_filter[l])
        act = jnp.tanh(preact[:, :channels])
        gate = 0.5 * jnp.tanh(0.5 * preact[:, channels:]) + 0.5
        gated = (act * gate).astype(BF16)
        stored.append((delayed, hidden, act, gate))
        hidden = (hidden + dot(gated, w_mixing[l])).astype(BF16).astype(F32)

    last = jnp.concatenate([hidden[b * span + HALO : (b + 1) * span] for b in range(seqs)], axis=0)
    last = last.astype(BF16)
    need("output")
    batch = 4 if scenarios % 4 == 0 else 1

    def columns(s):
        return pl.ds(pl.multiple_of(s * nodes, nodes), nodes)

    def predict(j, carry):
        for k in range(batch):
            s = j * batch + k
            pred = dot(last, w_output[:, columns(s)])
            for h in range(halves):
                scen[h, pl.ds(s, seqs * kept, stride=scenarios), :] = pred[:, h * 128 : (h + 1) * 128]
        return carry

    lax.fori_loop(0, scenarios // batch, predict, 0)
    need("obs")
    for b in range(seqs):
        scored[b * kept : b * kept + rows] = obs[b]
        scored[b * kept + rows : (b + 1) * kept] = next_obs[b]

    block = 16 * scenarios
    row_no = lax.broadcasted_iota(jnp.int32, (block, block), 0)
    col_no = lax.broadcasted_iota(jnp.int32, (block, block), 1)
    same_step = (row_no // scenarios) == (col_no // scenarios)
    diagonal = row_no == col_no
    pairs = jnp.where(same_step & ~diagonal, 1.0 / (scenarios * (scenarios - 1) * nodes), 0.0)

    def score(groups):
        ats = [pl.ds(pl.multiple_of(g * block, block), block) for g in groups]
        ys = [jnp.concatenate([scen[h, at, :] for h in range(halves)], axis=1) for at in ats]
        highs = [y.astype(BF16) for y in ys]
        lows = [(y - hi.astype(F32)).astype(BF16) for y, hi in zip(ys, highs)]
        grams = [
            dot(jnp.concatenate([hi, lo, hi, lo], axis=1), jnp.concatenate([hi, hi, lo, lo], axis=1), 1, 1)
            for hi, lo in zip(highs, lows)
        ]
        targets = []
        for g, y in zip(groups, ys):
            o = scored[pl.ds(pl.multiple_of(g * 16, 16), 16), :]
            diff = y - jnp.broadcast_to(o[:, None, :], (16, scenarios, nodes)).reshape(block, nodes)
            inv = lax.rsqrt(jnp.sum(diff * diff, axis=1, keepdims=True) * (1.0 / nodes) + epsilon)
            targets.append(inv * (1.0 / (scenarios * nodes)) * diff)
        coefs = []
        for gram in grams:
            own = jnp.where(diagonal, gram, 0.0)
            own_sq = jnp.sum(own, axis=1, keepdims=True) + jnp.sum(own, axis=0, keepdims=True)
            pair_sq = jnp.maximum(own_sq - 2.0 * gram, 0.0) * (1.0 / nodes)
            coefs.append(pairs * lax.rsqrt(pair_sq + epsilon))
        for at, y, hi, lo, coef, target in zip(ats, ys, highs, lows, coefs, targets):
            chi = coef.astype(BF16)
            clo = (coef - chi.astype(F32)).astype(BF16)
            mixed = dot(jnp.concatenate([chi, clo, chi], axis=1), jnp.concatenate([hi, hi, lo], axis=0))
            grad = mixed - jnp.sum(coef, axis=1, keepdims=True) * y + target
            for h in range(halves):
                scen[h, at, :] = grad[:, h * 128 : (h + 1) * 128]

    groups = seqs * kept // 16

    def score_pair(i, carry):
        score([2 * i, 2 * i + 1])
        return carry

    lax.fori_loop(0, groups // 2, score_pair, 0)
    if groups % 2:
        score([groups - 1])

    length = rows * nt
    step_no = lax.broadcasted_iota(jnp.int32, (kept, 1), 0)
    valid = jnp.where(step_no < rows, 1.0, not_last)
    factor = []
    total = need("total")
    for b in range(seqs):
        sq = jnp.sum(jnp.sum(total[b], axis=1, keepdims=True), axis=0, keepdims=True)
        factor.append(valid * lax.rsqrt(sq / (length * nodes) + epsilon))
    factor = jnp.concatenate(factor, axis=0)

    def kept_own(x):
        return jnp.concatenate([x[b * kept : b * kept + rows] for b in range(seqs)], axis=0)

    last_own = own_rows(hidden).T.astype(BF16)

    def output_step(j, grad_last):
        for k in range(batch):
            s = j * batch + k
            g = jnp.concatenate(
                [scen[h, pl.ds(s, seqs * kept, stride=scenarios), :] for h in range(halves)], axis=1
            )
            g = g * factor
            grad_last = grad_last + dot(g.astype(BF16), w_output[:, columns(s)], 1, 1)
            emit("output", (j, k), dot(last_own, kept_own(g).astype(BF16)))
        return grad_last

    grad_last = jnp.zeros((seqs * kept, channels), F32)
    grad_last = lax.fori_loop(0, scenarios // batch, output_step, grad_last)
    after("output")
    grad_last = grad_last.astype(BF16).astype(F32)
    pieces = []
    for b in range(seqs):
        pieces.append(jnp.zeros((HALO, channels), F32))
        pieces.append(grad_last[b * kept : (b + 1) * kept])
    grad = jnp.concatenate(pieces, axis=0)

    for l in reversed(range(layers)):
        delayed, held, act, gate = stored[l]
        grad16 = grad.astype(BF16)
        gated_t = own_rows(act * gate).T.astype(BF16)
        part = dot(gated_t, own_rows(grad).astype(BF16))
        emit("mixing", l, part)
        gated_cot = dot(grad16, w_mixing[l], 1, 1).astype(BF16).astype(F32)
        pre = jnp.concatenate(
            [gated_cot * gate * (1.0 - act * act), gated_cot * act * gate * (1.0 - gate)], axis=1
        )
        own_pre = own_rows(pre).astype(BF16)
        for tap, source in enumerate((delayed, held)):
            part = dot(own_rows(source).T.astype(BF16), own_pre)
            emit("filter", (l, tap), part)
        after(l)
        both = dot(pre.astype(BF16), w_filter[l], 1, 1).astype(BF16).astype(F32)
        past = pltpu.roll(both[:, :channels], seqs * span - 2**l, 0)
        grad = (grad + both[:, channels:] + past).astype(BF16).astype(F32)

    own = own_rows(grad).astype(BF16)
    cov_flat = jnp.concatenate([cov_own[b] for b in range(seqs)], axis=0)
    part = dot(cov_flat.astype(F32).T.astype(BF16), own)
    emit("input", None, part)
    after("input")
    result = dot(own, w_input[...], 1, 1).astype(BF16)
    for b in range(seqs):
        cov_grad[b] = result[b * rows : (b + 1) * rows]


def network_kernel(nt, cov, obs, prev_cov, next_cov, next_obs, total, *rest):
    weights, cov_grad, grads, (scen, scored) = rest[:4], rest[4], rest[5:9], rest[9:]
    g_input, g_filter, g_mixing, g_output = grads
    nodes, channels = cov.shape[2], weights[2].shape[1]

    def need(name):
        return total[...] if name == "total" else None

    def emit(name, index, part):
        part = part.astype(BF16)
        if name == "output":
            j, k = index
            batch = 4 if g_output.shape[1] // nodes % 4 == 0 else 1
            g_output[:, pl.ds(pl.multiple_of((j * batch + k) * nodes, nodes), nodes)] = part
        elif name == "mixing":
            g_mixing[index] = part
        elif name == "filter":
            l, tap = index
            g_filter[l, tap * channels : (tap + 1) * channels, :] = part
        else:
            g_input[...] = part

    network(
        nt, cov, obs, prev_cov, next_cov, next_obs, *weights, cov_grad, scen, scored,
        need, emit, lambda stage: None,
    )


def network_scratch(cov, w_output):
    seqs, rows, nodes = cov.shape
    steps = seqs * (rows + HALO)
    scenarios = w_output.shape[1] // nodes
    return [
        pltpu.VMEM((nodes // 128, steps * scenarios, 128), F32),
        pltpu.VMEM((steps, nodes), F32),
    ]


def run_network(nt, cov, obs, edges, weights):
    vmem = pl.BlockSpec(memory_space=pltpu.VMEM)
    grads = tuple(jax.ShapeDtypeStruct(w.shape, BF16) for w in weights)
    return pl.pallas_call(
        functools.partial(network_kernel, nt),
        out_shape=(jax.ShapeDtypeStruct(cov.shape, BF16),) + grads,
        in_specs=[vmem] * 10,
        out_specs=(vmem,) * (1 + len(grads)),
        scratch_shapes=network_scratch(cov, weights[3]),
        compiler_params=pltpu.CompilerParams(vmem_limit_bytes=56 * 2**20),
        name="network",
    )(cov, obs, *edges, *weights)


def bit_dims(nt, nr):
    bits = lambda n: n.bit_length() - 1
    tm_dims = [("tm", 2**i) for i in reversed(range(bits(nt)))]
    region_dims = [("region", 2**i) for i in reversed(range(bits(nr)))]
    return tm_dims, region_dims


def orders_of(tm_dims, region_dims):
    near = region_dims[-1:]
    x, ys = region_dims[:-1], list(reversed(tm_dims))
    y, z = ys[:1], ys[1:]

    def twos(dims):
        return [dims[i : i + 2] for i in range(0, len(dims), 2)]

    orders = [
        [near, x, y] + twos(z),
        [near, y, x] + twos(z),
        [near, z[:1], x, y + z[1:2]] + twos(z[2:]),
    ]
    return [[group for group in order if group] for order in orders]


def even_parts(rows, orders):
    units = rows // 16
    count = min(2 * len(orders), units)
    cuts = [16 * (units * i // count) for i in range(count + 1)]
    return [(cuts[i], cuts[i + 1] - cuts[i], orders[i % 3]) for i in range(count)]


class Halving:
    def __init__(self, sources, tm_dims, region_dims, parts, buffers, whole, send_sem, recv_sem):
        self.region_dims, self.parts = region_dims, parts
        self.whole = whole
        self.send_sem, self.recv_sem = send_sem, recv_sem
        self.current = list(sources)
        buffers = list(buffers)
        self.buffers = [[buffers.pop(0) for _ in order] for _, _, order in parts]
        self.phase = [0 for _ in parts]
        self.flying = [[] for _ in parts]
        self.done = []
        self.slot = 0
        self.where = {"tm": lax.axis_index("tm"), "region": lax.axis_index("region")}

    def bit(self, dim):
        axis, weight = dim
        return lax.rem(lax.div(self.where[axis], weight), 2)

    def partners(self, group):
        masks = range(1, 2 ** len(group))
        return [[d for n, d in enumerate(group) if mask >> n & 1] for mask in masks]

    def across(self, dims):
        place = {}
        for axis, weight in dims:
            here = place.get(axis, self.where[axis])
            place[axis] = here + weight * (1 - 2 * self.bit((axis, weight)))
        return place

    def greet(self, barrier):
        met = {}
        for group in [g for _, _, order in self.parts for g in order] + [self.region_dims]:
            for dims in self.partners(group):
                met[tuple(sorted(dims))] = dims
        for key in sorted(met):
            pl.semaphore_signal(barrier, inc=1, device_id=self.across(met[key]), device_id_type=MESH)
        return len(met)

    def copy(self, i, src, dst, dims):
        copy = pltpu.make_async_remote_copy(
            src_ref=src, dst_ref=dst,
            send_sem=self.send_sem.at[self.slot], recv_sem=self.recv_sem.at[self.slot],
            device_id=self.across(dims), device_id_type=MESH,
        )
        self.slot += 1
        copy.start()
        self.flying[i].append(copy)

    def send_part(self, i):
        group = self.parts[i][2][self.phase[i]]
        for n, dims in enumerate(self.partners(group)):
            index = tuple(1 - self.bit(d) if d in dims else self.bit(d) for d in group)
            self.copy(i, self.current[i].at[index], self.buffers[i][self.phase[i]].at[n], dims)

    def send_sum(self, i):
        start, height, _ = self.parts[i]
        index = tuple(self.bit(d) for d in self.region_dims) + (pl.ds(start, height), slice(None))
        self.whole[index] = self.current[i][...]
        for dims in self.partners(self.region_dims):
            self.copy(i, self.whole.at[index], self.whole.at[index], dims)

    def advance(self, i):
        if not self.flying[i]:
            return False
        for copy in self.flying[i]:
            copy.wait_recv()
        self.done += self.flying[i]
        self.flying[i] = []
        phase, order = self.phase[i], self.parts[i][2]
        self.phase[i] += 1
        if phase < len(order):
            buffer = self.buffers[i][phase]
            total = self.current[i][tuple(self.bit(d) for d in order[phase])].astype(F32)
            for n in range(buffer.shape[0]):
                total = total + buffer[n].astype(F32)
            buffer[0] = total.astype(BF16)
            self.current[i] = buffer.at[0]
            if phase + 1 < len(order):
                self.send_part(i)
            else:
                self.send_sum(i)
        return True

    def finish(self):
        while any([self.advance(i) for i in range(len(self.parts))]):
            pass
        for copy in self.done:
            copy.wait_send()


def halving_scratch(region_dims, parts, rows, nodes):
    scratch, copies = [], 0
    for _, height, order in parts:
        left = sum(len(group) for group in order)
        for group in order:
            left -= len(group)
            others = 2 ** len(group) - 1
            scratch.append(pltpu.VMEM((others,) + (2,) * left + (height, nodes), BF16))
            copies += others
        copies += 2 ** len(region_dims) - 1
    return scratch, [
        pltpu.VMEM((2,) * len(region_dims) + (rows, nodes), BF16),
        pltpu.SemaphoreType.DMA((copies,)),
        pltpu.SemaphoreType.DMA((copies,)),
    ]


def flat(order):
    return [d for group in order for d in group]


def reduce_kernel(tm_dims, region_dims, parts, *refs):
    sources, out, refs = refs[: len(parts)], refs[len(parts)], refs[len(parts) + 1 :]
    halving = Halving(sources, tm_dims, region_dims, parts, refs[:-3], *refs[-3:])
    barrier = pltpu.get_barrier_semaphore()
    met = halving.greet(barrier)
    pl.semaphore_wait(barrier, met)
    for i in range(len(parts)):
        halving.send_part(i)
    halving.finish()
    out[...] = halving.whole[...]


def reduce_grads(tm_dims, region_dims, parts, rows, sources):
    nodes = sources[0].shape[-1]
    buffers, ends = halving_scratch(region_dims, parts, rows, nodes)
    vmem = pl.BlockSpec(memory_space=pltpu.VMEM)
    return pl.pallas_call(
        functools.partial(reduce_kernel, tm_dims, region_dims, parts),
        out_shape=jax.ShapeDtypeStruct((2,) * len(region_dims) + (rows, nodes), BF16),
        in_specs=[vmem] * len(sources),
        out_specs=vmem,
        scratch_shapes=buffers + ends,
        compiler_params=pltpu.CompilerParams(
            collective_id=1, has_side_effects=True, vmem_limit_bytes=56 * 2**20
        ),
        name="reduce",
    )(*sources)


def split_parts(grads, dims, parts):
    sources = []
    for start, height, order in parts:
        moved = tuple(dims.index(d) for d in flat(order)) + (len(dims), len(dims) + 1)
        sources.append(jnp.transpose(grads[..., start : start + height, :], moved))
    return sources


def packed_kernel(nt, parts, cov, obs, prev_cov, next_cov, next_obs, total, *rest):
    weights, cov_grad, sources, (scen, scored) = rest[:4], rest[4], rest[5:-2], rest[-2:]
    nodes = cov.shape[2]
    layers, channels = weights[2].shape[:2]
    unit = channels // nt
    per = weights[3].shape[1] // nodes // 4
    every = range(nt)

    def need(name):
        return total[...] if name == "total" else None

    def put(owners, sub, at, value):
        value = value.reshape(len(owners), unit, nodes).astype(BF16)
        place = {("region", 2): lax.div(sub, 2), ("region", 1): lax.rem(sub, 2)}
        for source, (start, height, order) in zip(sources, parts):
            low, high = max(start, at * unit), min(start + height, (at + 1) * unit)
            if low >= high:
                continue
            for j, owner in enumerate(owners):
                index = tuple(place[d] if d in place else owner // d[1] % 2 for d in flat(order))
                index = index + (slice(low - start, high - start), slice(None))
                source[index] = value[j, low - at * unit : high - at * unit]

    def emit(name, index, part):
        if name == "output":
            put(every, index[0], index[1], part)
        elif name == "mixing":
            put(every, index, per + layers, part)
        elif name == "input":
            put(every, layers, per + layers, part)
        else:
            l, tap = index
            owners = range(tap * nt // 2, (tap + 1) * nt // 2)
            for h in range(2):
                piece = part[:, h * nodes : (h + 1) * nodes].reshape(nt // 2, 2, unit, nodes)
                for q in range(2):
                    put(owners, h * 2 + q, per + layers - 1 - l, piece[:, q])

    network(
        nt, cov, obs, prev_cov, next_cov, next_obs, *weights, cov_grad, scen, scored,
        need, emit, lambda stage: None,
    )


def run_packed(nt, dims, parts, cov, obs, edges, weights):
    vmem = pl.BlockSpec(memory_space=pltpu.VMEM)
    nodes = cov.shape[2]
    sources = tuple(
        jax.ShapeDtypeStruct((2,) * len(dims) + (height, nodes), BF16) for _, height, _ in parts
    )
    return pl.pallas_call(
        functools.partial(packed_kernel, nt, parts),
        out_shape=(jax.ShapeDtypeStruct(cov.shape, BF16),) + sources,
        in_specs=[vmem] * 10,
        out_specs=(vmem,) * (1 + len(sources)),
        scratch_shapes=network_scratch(cov, weights[3]),
        compiler_params=pltpu.CompilerParams(vmem_limit_bytes=56 * 2**20),
        name="network",
    )(cov, obs, *edges, *weights)


def unpack_kernel(whole, o_input, o_filter, o_mixing, o_output):
    unit, nodes = o_input.shape
    layers = o_filter.shape[0]
    scenarios = o_output.shape[1] // nodes
    per = scenarios // 4

    def piece(sub, at):
        return whole[sub // 2, sub % 2, at * unit : (at + 1) * unit, :]

    for s in range(scenarios):
        o_output[:, s * nodes : (s + 1) * nodes] = piece(s // per, s % per)
    for l in range(layers):
        for h in range(2):
            for q in range(2):
                o_filter[l, q * unit : (q + 1) * unit, h * nodes : (h + 1) * nodes] = piece(
                    h * 2 + q, per + layers - 1 - l
                )
        o_mixing[l] = piece(l, per + layers)
    o_input[...] = piece(layers, per + layers)


def unpack(summed, shapes):
    vmem = pl.BlockSpec(memory_space=pltpu.VMEM)
    return pl.pallas_call(
        unpack_kernel,
        out_shape=tuple(jax.ShapeDtypeStruct(s, BF16) for s in shapes),
        in_specs=[vmem],
        out_specs=(vmem,) * len(shapes),
        name="unpack",
    )(summed)


def per_device(nt, nr, cov, obs, w_input, w_filter, w_mixing, w_output):
    nodes = cov.shape[2]
    weights = (w_input, w_filter, w_mixing, w_output)
    layers, channels = w_mixing.shape[:2]
    scenarios = w_output.shape[1] // nodes
    unit = channels // nt
    shapes = (
        (unit, nodes), (layers, 2 * unit, 2 * channels), (layers, unit, channels), (unit, scenarios * nodes)
    )
    tm_dims, region_dims = bit_dims(nt, nr)
    dims = tm_dims + region_dims
    rows = sum(w.size for w in weights) // nt // nodes // nr
    parts = even_parts(rows, orders_of(tm_dims, region_dims))
    edges = exchange_edges(nt, cov, obs)
    if unit % 16 == 0 and nr == 4 and layers == 3 and scenarios == 16 and channels == nodes:
        cov_grad, *sources = run_packed(nt, dims, parts, cov, obs, edges, weights)
        summed = reduce_grads(tm_dims, region_dims, parts, rows, sources)
        return (cov_grad, *unpack(summed, shapes))
    cov_grad, *grads = run_network(nt, cov, obs, edges, weights)
    sources = tuple(
        jnp.moveaxis(g.reshape(g.shape[:-2] + (nt, -1) + g.shape[-1:]), -3, 0) for g in grads
    )
    together = jnp.concatenate([s.reshape(nt, -1) for s in sources], axis=1)
    together = together.reshape((2,) * len(dims) + (rows, nodes))
    summed = reduce_grads(tm_dims, region_dims, parts, rows, split_parts(together, dims, parts))
    summed = summed.reshape(-1)
    outs, first = [], 0
    for source, shape in zip(sources, shapes):
        size = source.size // nt
        outs.append(summed[first : first + size].reshape(shape))
        first += size
    return (cov_grad, *outs)


def solution(mesh):
    placed = (P("region", "tm", None), P("region", "tm", None), P(), P(), P(), P())
    return jax.shard_map(
        functools.partial(per_device, mesh.shape["tm"], mesh.shape["region"]),
        mesh=mesh,
        in_specs=placed,
        out_specs=(
            P("region", "tm", None),
            P("tm", None),
            P(None, "tm", None),
            P(None, "tm", None),
            P("tm", None),
        ),
        check_vma=False,
    )
```

```python
import functools

import jax
import jax.numpy as jnp
from jax import lax
from jax.experimental import pallas as pl
from jax.experimental.pallas import tpu as pltpu
from jax.sharding import PartitionSpec as P

MESH = pl.DeviceIdType.MESH
epsilon = 1e-05
HALO = 8
F32 = jnp.float32
BF16 = jnp.bfloat16


def dot(a, b, ca=1, cb=0, precision=None):
    return lax.dot_general(
        a, b, (((ca,), (cb,)), ((), ())), precision=precision, preferred_element_type=F32
    )


class Edges:
    def __init__(self, nt, cov, obs, got_prev, got_next, got_obs, sums, send_sem, recv_sem):
        self.nt, self.cov, self.obs, self.sums = nt, cov, obs, sums
        self.got = (got_prev, got_next, got_obs)
        self.send_sem, self.recv_sem = send_sem, recv_sem
        self.copies = []

    def at(self, offset):
        return {"tm": lax.rem(lax.axis_index("tm") + offset, self.nt)}

    def greet(self, barrier):
        for offset in range(1, self.nt):
            pl.semaphore_signal(barrier, inc=1, device_id=self.at(offset), device_id_type=MESH)

    def own_squares(self):
        seqs, rows, nodes = self.obs.shape
        sq = self.obs[...] * self.obs[...]
        sq = jnp.sum(sq.reshape(seqs, rows // 8, 8, nodes), axis=1)
        own = sq[:, :, :128]
        for part in range(1, nodes // 128):
            own = own + sq[:, :, part * 128 : (part + 1) * 128]
        self.sums[0] = own

    def send(self, src, dst, offset):
        slot = len(self.copies)
        copy = pltpu.make_async_remote_copy(
            src_ref=src, dst_ref=dst,
            send_sem=self.send_sem.at[slot], recv_sem=self.recv_sem.at[slot],
            device_id=self.at(offset), device_id_type=MESH,
        )
        copy.start()
        self.copies.append(copy)

    def start(self):
        nt, rows = self.nt, self.cov.shape[1]
        self.send(self.cov.at[:, pl.ds(rows - 16, 16), :], self.got[0], 1)
        self.send(self.cov.at[:, pl.ds(0, 16), :], self.got[1], nt - 1)
        self.send(self.obs.at[:, pl.ds(0, HALO), :], self.got[2], nt - 1)
        for offset in range(1, nt):
            self.send(self.sums.at[0], self.sums.at[offset], offset)

    def arrived(self, first, last):
        for copy in self.copies[first:last]:
            copy.wait_recv()

    def sent(self):
        for copy in self.copies:
            copy.wait_send()

    def total(self):
        return jnp.sum(self.sums[...], axis=0)


def edges_kernel(nt, cov, obs, prev_cov, next_cov, next_obs, total, *scratch):
    edges = Edges(nt, cov, obs, *scratch)
    barrier = pltpu.get_barrier_semaphore()
    edges.greet(barrier)
    edges.own_squares()
    pl.semaphore_wait(barrier, nt - 1)
    edges.start()
    edges.arrived(0, None)
    edges.sent()
    for out, got in zip((prev_cov, next_cov, next_obs), edges.got):
        out[...] = got[...]
    total[...] = edges.total()


def exchange_edges(nt, cov, obs):
    seqs, rows, nodes = cov.shape
    vmem = pl.BlockSpec(memory_space=pltpu.VMEM)
    edge = jax.ShapeDtypeStruct((seqs, 16, nodes), BF16)
    copies = nt + 2
    return pl.pallas_call(
        functools.partial(edges_kernel, nt),
        out_shape=(
            edge,
            edge,
            jax.ShapeDtypeStruct((seqs, HALO, nodes), F32),
            jax.ShapeDtypeStruct((seqs, 8, 128), F32),
        ),
        in_specs=[vmem] * 2,
        out_specs=(vmem,) * 4,
        scratch_shapes=[
            pltpu.VMEM((seqs, 16, nodes), BF16),
            pltpu.VMEM((seqs, 16, nodes), BF16),
            pltpu.VMEM((seqs, HALO, nodes), F32),
            pltpu.VMEM((nt, seqs, 8, 128), F32),
            pltpu.SemaphoreType.DMA((copies,)),
            pltpu.SemaphoreType.DMA((copies,)),
        ],
        compiler_params=pltpu.CompilerParams(collective_id=0, has_side_effects=True),
        name="edges",
    )(cov, obs)


def network(
    nt, cov, obs, prev_cov, next_cov, next_obs, w_input, w_filter, w_mixing, w_output,
    cov_grad, scen, scored, need, emit, after,
):
    me = lax.axis_index("tm")
    seqs, rows, nodes = cov.shape
    layers = w_filter.shape[0]
    channels = w_mixing.shape[1]
    scenarios = w_output.shape[1] // nodes
    span = rows + 2 * HALO
    kept = rows + HALO
    halves = nodes // 128
    not_first = (me > 0).astype(F32)
    not_last = (me < nt - 1).astype(F32)

    def own_rows(x):
        return jnp.concatenate([x[b * span + HALO : b * span + HALO + rows] for b in range(seqs)], axis=0)

    cov_own = cov[...]
    need("cov")
    need("input")
    spans = []
    for b in range(seqs):
        spans.append(prev_cov[b].astype(F32)[16 - HALO :] * not_first)
        spans.append(cov_own[b].astype(F32))
        spans.append(next_cov[b].astype(F32)[:HALO])
    hidden = dot(jnp.concatenate(spans, axis=0).astype(BF16), w_input[...]).astype(BF16).astype(F32)
    stored = []
    need("filter")
    need("mixing")
    for l in range(layers):
        delayed = pltpu.roll(hidden, 2**l, 0)
        joined = jnp.concatenate([delayed, hidden], axis=1).astype(BF16)
        preact = dot(joined, w_filter[l])
        act = jnp.tanh(preact[:, :channels])
        gate = 0.5 * jnp.tanh(0.5 * preact[:, channels:]) + 0.5
        gated = (act * gate).astype(BF16)
        stored.append((delayed, hidden, act, gate))
        hidden = (hidden + dot(gated, w_mixing[l])).astype(BF16).astype(F32)

    last = jnp.concatenate([hidden[b * span + HALO : (b + 1) * span] for b in range(seqs)], axis=0)
    last = last.astype(BF16)
    need("output")
    batch = 4 if scenarios % 4 == 0 else 1

    def columns(s):
        return pl.ds(pl.multiple_of(s * nodes, nodes), nodes)

    def predict(j, carry):
        for k in range(batch):
            s = j * batch + k
            pred = dot(last, w_output[:, columns(s)])
            for h in range(halves):
                scen[h, pl.ds(s, seqs * kept, stride=scenarios), :] = pred[:, h * 128 : (h + 1) * 128]
        return carry

    lax.fori_loop(0, scenarios // batch, predict, 0)
    need("obs")
    for b in range(seqs):
        scored[b * kept : b * kept + rows] = obs[b]
        scored[b * kept + rows : (b + 1) * kept] = next_obs[b]

    block = 16 * scenarios
    row_no = lax.broadcasted_iota(jnp.int32, (block, block), 0)
    col_no = lax.broadcasted_iota(jnp.int32, (block, block), 1)
    same_step = (row_no // scenarios) == (col_no // scenarios)
    diagonal = row_no == col_no
    pairs = jnp.where(same_step & ~diagonal, 1.0 / (scenarios * (scenarios - 1) * nodes), 0.0)

    def score(groups):
        ats = [pl.ds(pl.multiple_of(g * block, block), block) for g in groups]
        ys = [jnp.concatenate([scen[h, at, :] for h in range(halves)], axis=1) for at in ats]
        highs = [y.astype(BF16) for y in ys]
        lows = [(y - hi.astype(F32)).astype(BF16) for y, hi in zip(ys, highs)]
        grams = [
            dot(jnp.concatenate([hi, lo, hi, lo], axis=1), jnp.concatenate([hi, hi, lo, lo], axis=1), 1, 1)
            for hi, lo in zip(highs, lows)
        ]
        targets = []
        for g, y in zip(groups, ys):
            o = scored[pl.ds(pl.multiple_of(g * 16, 16), 16), :]
            diff = y - jnp.broadcast_to(o[:, None, :], (16, scenarios, nodes)).reshape(block, nodes)
            inv = lax.rsqrt(jnp.sum(diff * diff, axis=1, keepdims=True) * (1.0 / nodes) + epsilon)
            targets.append(inv * (1.0 / (scenarios * nodes)) * diff)
        coefs = []
        for gram in grams:
            own = jnp.where(diagonal, gram, 0.0)
            own_sq = jnp.sum(own, axis=1, keepdims=True) + jnp.sum(own, axis=0, keepdims=True)
            pair_sq = jnp.maximum(own_sq - 2.0 * gram, 0.0) * (1.0 / nodes)
            coefs.append(pairs * lax.rsqrt(pair_sq + epsilon))
        for at, y, hi, lo, coef, target in zip(ats, ys, highs, lows, coefs, targets):
            chi = coef.astype(BF16)
            clo = (coef - chi.astype(F32)).astype(BF16)
            mixed = dot(jnp.concatenate([chi, clo, chi], axis=1), jnp.concatenate([hi, hi, lo], axis=0))
            grad = mixed - jnp.sum(coef, axis=1, keepdims=True) * y + target
            for h in range(halves):
                scen[h, at, :] = grad[:, h * 128 : (h + 1) * 128]

    groups = seqs * kept // 16

    def score_pair(i, carry):
        score([2 * i, 2 * i + 1])
        return carry

    lax.fori_loop(0, groups // 2, score_pair, 0)
    if groups % 2:
        score([groups - 1])

    length = rows * nt
    step_no = lax.broadcasted_iota(jnp.int32, (kept, 1), 0)
    valid = jnp.where(step_no < rows, 1.0, not_last)
    factor = []
    total = need("total")
    for b in range(seqs):
        sq = jnp.sum(jnp.sum(total[b], axis=1, keepdims=True), axis=0, keepdims=True)
        factor.append(valid * lax.rsqrt(sq / (length * nodes) + epsilon))
    factor = jnp.concatenate(factor, axis=0)

    def kept_own(x):
        return jnp.concatenate([x[b * kept : b * kept + rows] for b in range(seqs)], axis=0)

    last_own = own_rows(hidden).T.astype(BF16)

    def output_step(j, grad_last):
        for k in range(batch):
            s = j * batch + k
            g = jnp.concatenate(
                [scen[h, pl.ds(s, seqs * kept, stride=scenarios), :] for h in range(halves)], axis=1
            )
            g = g * factor
            grad_last = grad_last + dot(g.astype(BF16), w_output[:, columns(s)], 1, 1)
            emit("output", (j, k), dot(last_own, kept_own(g).astype(BF16)))
        return grad_last

    grad_last = jnp.zeros((seqs * kept, channels), F32)
    grad_last = lax.fori_loop(0, scenarios // batch, output_step, grad_last)
    after("output")
    grad_last = grad_last.astype(BF16).astype(F32)
    pieces = []
    for b in range(seqs):
        pieces.append(jnp.zeros((HALO, channels), F32))
        pieces.append(grad_last[b * kept : (b + 1) * kept])
    grad = jnp.concatenate(pieces, axis=0)

    for l in reversed(range(layers)):
        delayed, held, act, gate = stored[l]
        grad16 = grad.astype(BF16)
        gated_t = own_rows(act * gate).T.astype(BF16)
        part = dot(gated_t, own_rows(grad).astype(BF16))
        emit("mixing", l, part)
        gated_cot = dot(grad16, w_mixing[l], 1, 1).astype(BF16).astype(F32)
        pre = jnp.concatenate(
            [gated_cot * gate * (1.0 - act * act), gated_cot * act * gate * (1.0 - gate)], axis=1
        )
        own_pre = own_rows(pre).astype(BF16)
        for tap, source in enumerate((delayed, held)):
            part = dot(own_rows(source).T.astype(BF16), own_pre)
            emit("filter", (l, tap), part)
        after(l)
        both = dot(pre.astype(BF16), w_filter[l], 1, 1).astype(BF16).astype(F32)
        past = pltpu.roll(both[:, :channels], seqs * span - 2**l, 0)
        grad = (grad + both[:, channels:] + past).astype(BF16).astype(F32)

    own = own_rows(grad).astype(BF16)
    cov_flat = jnp.concatenate([cov_own[b] for b in range(seqs)], axis=0)
    part = dot(cov_flat.astype(F32).T.astype(BF16), own)
    emit("input", None, part)
    after("input")
    result = dot(own, w_input[...], 1, 1).astype(BF16)
    for b in range(seqs):
        cov_grad[b] = result[b * rows : (b + 1) * rows]


def network_kernel(nt, cov, obs, prev_cov, next_cov, next_obs, total, *rest):
    weights, cov_grad, grads, (scen, scored) = rest[:4], rest[4], rest[5:9], rest[9:]
    g_input, g_filter, g_mixing, g_output = grads
    nodes, channels = cov.shape[2], weights[2].shape[1]

    def need(name):
        return total[...] if name == "total" else None

    def emit(name, index, part):
        part = part.astype(BF16)
        if name == "output":
            j, k = index
            batch = 4 if g_output.shape[1] // nodes % 4 == 0 else 1
            g_output[:, pl.ds(pl.multiple_of((j * batch + k) * nodes, nodes), nodes)] = part
        elif name == "mixing":
            g_mixing[index] = part
        elif name == "filter":
            l, tap = index
            g_filter[l, tap * channels : (tap + 1) * channels, :] = part
        else:
            g_input[...] = part

    network(
        nt, cov, obs, prev_cov, next_cov, next_obs, *weights, cov_grad, scen, scored,
        need, emit, lambda stage: None,
    )


def network_scratch(cov, w_output):
    seqs, rows, nodes = cov.shape
    steps = seqs * (rows + HALO)
    scenarios = w_output.shape[1] // nodes
    return [
        pltpu.VMEM((nodes // 128, steps * scenarios, 128), F32),
        pltpu.VMEM((steps, nodes), F32),
    ]


def run_network(nt, cov, obs, edges, weights):
    vmem = pl.BlockSpec(memory_space=pltpu.VMEM)
    grads = tuple(jax.ShapeDtypeStruct(w.shape, BF16) for w in weights)
    return pl.pallas_call(
        functools.partial(network_kernel, nt),
        out_shape=(jax.ShapeDtypeStruct(cov.shape, BF16),) + grads,
        in_specs=[vmem] * 10,
        out_specs=(vmem,) * (1 + len(grads)),
        scratch_shapes=network_scratch(cov, weights[3]),
        compiler_params=pltpu.CompilerParams(vmem_limit_bytes=56 * 2**20),
        name="network",
    )(cov, obs, *edges, *weights)


def bit_dims(nt, nr):
    bits = lambda n: n.bit_length() - 1
    tm_dims = [("tm", 2**i) for i in reversed(range(bits(nt)))]
    region_dims = [("region", 2**i) for i in reversed(range(bits(nr)))]
    return tm_dims, region_dims


def orders_of(tm_dims, region_dims):
    near = region_dims[-1:]
    x, ys = region_dims[:-1], list(reversed(tm_dims))
    y, z = ys[:1], ys[1:]
    return [near + x + y + z, near + y + z[:1] + x + z[1:], near + z[:1] + x + y + z[1:]]


def even_parts(rows, orders):
    units = rows // 16
    count = min(2 * len(orders), units)
    cuts = [16 * (units * i // count) for i in range(count + 1)]
    return [(cuts[i], cuts[i + 1] - cuts[i], orders[i % 3]) for i in range(count)]


class Halving:
    def __init__(self, sources, tm_dims, region_dims, parts, buffers, whole, send_sem, recv_sem):
        self.dims, self.region_dims, self.parts = tm_dims + region_dims, region_dims, parts
        self.whole = whole
        self.send_sem, self.recv_sem = send_sem, recv_sem
        n = len(self.dims)
        self.buffers = [buffers[i * n : (i + 1) * n] for i in range(len(parts))]
        self.current = list(sources)
        self.phase = [0 for _ in parts]
        self.flying = [None for _ in parts]
        self.done = []
        self.slot = 0
        self.where = {"tm": lax.axis_index("tm"), "region": lax.axis_index("region")}

    def bit(self, dim):
        axis, weight = dim
        return lax.rem(lax.div(self.where[axis], weight), 2)

    def across(self, dim):
        axis, weight = dim
        return {axis: self.where[axis] + weight * (1 - 2 * self.bit(dim))}

    def copy(self, i, src, dst, dim):
        copy = pltpu.make_async_remote_copy(
            src_ref=src, dst_ref=dst,
            send_sem=self.send_sem.at[self.slot], recv_sem=self.recv_sem.at[self.slot],
            device_id=self.across(dim), device_id_type=MESH,
        )
        self.slot += 1
        copy.start()
        self.flying[i] = copy

    def rows_at(self, i):
        return pl.ds(self.parts[i][0], self.parts[i][1])

    def send_half(self, i):
        dim = self.parts[i][2][self.phase[i]]
        self.copy(i, self.current[i].at[1 - self.bit(dim)], self.buffers[i][self.phase[i]], dim)

    def send_whole(self, i, n):
        index = tuple(slice(None) if m < n else self.bit(d) for m, d in enumerate(self.region_dims))
        index = index + (self.rows_at(i), slice(None))
        self.copy(i, self.whole.at[index], self.whole.at[index], self.region_dims[n])

    def begin(self, i):
        self.send_half(i)

    def advance(self, i):
        if self.flying[i] is None:
            return False
        self.flying[i].wait_recv()
        self.done.append(self.flying[i])
        self.flying[i] = None
        phase, last = self.phase[i], len(self.dims)
        if phase < last:
            dim = self.parts[i][2][phase]
            into = self.buffers[i][phase]
            mine = self.current[i][self.bit(dim)]
            into[...] = (into[...].astype(F32) + mine.astype(F32)).astype(BF16)
            self.current[i] = into
            self.phase[i] += 1
            if phase + 1 < last:
                self.send_half(i)
            else:
                index = tuple(self.bit(d) for d in self.region_dims)
                self.whole[index + (self.rows_at(i), slice(None))] = into[...]
                self.send_whole(i, 0)
        else:
            self.phase[i] += 1
            if phase + 1 - last < len(self.region_dims):
                self.send_whole(i, phase + 1 - last)
        return True

    def round(self):
        return any([self.advance(i) for i in range(len(self.parts))])

    def finish(self):
        while self.round():
            pass
        for copy in self.done:
            copy.wait_send()


def halving_scratch(tm_dims, region_dims, parts, rows, nodes):
    n = len(tm_dims) + len(region_dims)
    scratch = []
    for _, height, _ in parts:
        for phase in range(n):
            scratch.append(pltpu.VMEM((2,) * (n - phase - 1) + (height, nodes), BF16))
    copies = len(parts) * (n + len(region_dims))
    return scratch, [
        pltpu.VMEM((2,) * len(region_dims) + (rows, nodes), BF16),
        pltpu.SemaphoreType.DMA((copies,)),
        pltpu.SemaphoreType.DMA((copies,)),
    ]


def reduce_kernel(tm_dims, region_dims, parts, *refs):
    sources, out, refs = refs[: len(parts)], refs[len(parts)], refs[len(parts) + 1 :]
    halving = Halving(sources, tm_dims, region_dims, parts, refs[:-3], *refs[-3:])
    barrier = pltpu.get_barrier_semaphore()
    for dim in halving.dims:
        pl.semaphore_signal(barrier, inc=1, device_id=halving.across(dim), device_id_type=MESH)
    pl.semaphore_wait(barrier, len(halving.dims))
    for i in range(len(parts)):
        halving.begin(i)
    halving.finish()
    out[...] = halving.whole[...]


def reduce_grads(nt, nr, grads):
    _, width, nodes = grads.shape
    rows = width // nr
    tm_dims, region_dims = bit_dims(nt, nr)
    parts = even_parts(rows, orders_of(tm_dims, region_dims))
    grads = grads.reshape((2,) * (len(tm_dims) + len(region_dims)) + (rows, nodes))
    dims = tm_dims + region_dims
    sources = []
    for start, height, order in parts:
        moved = tuple(dims.index(d) for d in order) + (len(dims), len(dims) + 1)
        sources.append(jnp.transpose(grads[..., start : start + height, :], moved))
    buffers, ends = halving_scratch(tm_dims, region_dims, parts, rows, nodes)
    vmem = pl.BlockSpec(memory_space=pltpu.VMEM)
    return pl.pallas_call(
        functools.partial(reduce_kernel, tm_dims, region_dims, parts),
        out_shape=jax.ShapeDtypeStruct((2,) * len(region_dims) + (rows, nodes), BF16),
        in_specs=[vmem] * len(sources),
        out_specs=vmem,
        scratch_shapes=buffers + ends,
        compiler_params=pltpu.CompilerParams(
            collective_id=1, has_side_effects=True, vmem_limit_bytes=56 * 2**20
        ),
        name="reduce",
    )(*sources)


def staged_parts(unit, layers, per, orders):
    by_x, by_y, by_z = orders
    third = per * unit // 3 // 16 * 16
    early = per * unit - 2 * third
    parts, stages = [], {}

    def add(stage, start, height, order):
        stages.setdefault(stage, []).append(len(parts))
        parts.append((start, height, order))

    add("output", 0, early - (early - third) // 2 // 16 * 16, by_x)
    second = parts[0][1]
    add("output", second, per * unit - second - third, by_y)
    add("output", per * unit - third, third, by_z)
    early_layers = (layers + 1) // 2
    add(layers - early_layers, per * unit, early_layers * unit, by_z)
    tail = (per + early_layers) * unit
    rest = (layers + 1 - early_layers) * unit
    cut = rest // 2 // 16 * 16
    add("input", tail, cut, by_x)
    add("input", tail + cut, rest - cut, by_y)
    return parts, stages


def step_kernel(
    nt, tm_dims, region_dims, parts, stages,
    cov, obs, w_input, w_filter, w_mixing, w_output, cov_grad, out,
    scen, scored, v_input, v_filter, v_mixing, v_output, load_sem, *refs,
):
    edges = Edges(nt, cov, obs, *refs[:6])
    sources, refs = refs[6 : 6 + len(parts)], refs[len(parts) :]
    halving = Halving(sources, tm_dims, region_dims, parts, refs[6:-3], *refs[-3:])
    barrier = pltpu.get_barrier_semaphore()
    edges.greet(barrier)
    for dim in region_dims:
        pl.semaphore_signal(barrier, inc=1, device_id=halving.across(dim), device_id_type=MESH)
    loads = {}
    pairs = (("input", w_input, v_input), ("filter", w_filter, v_filter),
             ("mixing", w_mixing, v_mixing), ("output", w_output, v_output))
    for n, (name, src, dst) in enumerate(pairs):
        loads[name] = pltpu.make_async_copy(src, dst, load_sem.at[n])
        loads[name].start()
    edges.own_squares()
    pl.semaphore_wait(barrier, nt - 1 + len(region_dims))
    edges.start()

    nodes = cov.shape[2]
    layers, channels = w_mixing.shape[:2]
    unit = channels // nt
    per = w_output.shape[1] // nodes // 4
    every = range(nt)

    def need(name):
        if name == "cov":
            edges.arrived(0, 2)
        elif name == "obs":
            edges.arrived(2, 3)
        elif name == "total":
            edges.arrived(3, None)
            return edges.total()
        else:
            loads[name].wait()

    def put(owners, sub, at, value):
        value = value.reshape(len(owners), unit, nodes).astype(BF16)
        place = {("region", 2): lax.div(sub, 2), ("region", 1): lax.rem(sub, 2)}
        for source, (start, height, order) in zip(sources, parts):
            low, high = max(start, at * unit), min(start + height, (at + 1) * unit)
            if low >= high:
                continue
            for j, owner in enumerate(owners):
                index = tuple(place[d] if d in place else owner // d[1] % 2 for d in order)
                index = index + (slice(low - start, high - start), slice(None))
                source[index] = value[j, low - at * unit : high - at * unit]

    def emit(name, index, part):
        if name == "output":
            put(every, index[0], index[1], part)
        elif name == "mixing":
            put(every, index, per + layers, part)
        elif name == "input":
            put(every, layers, per + layers, part)
        else:
            l, tap = index
            owners = range(tap * nt // 2, (tap + 1) * nt // 2)
            for h in range(2):
                piece = part[:, h * nodes : (h + 1) * nodes].reshape(nt // 2, 2, unit, nodes)
                for q in range(2):
                    put(owners, h * 2 + q, per + layers - 1 - l, piece[:, q])

    def after(stage):
        for i in stages.get(stage, []):
            halving.begin(i)

    network(
        nt, cov, obs, *edges.got, v_input, v_filter, v_mixing, v_output, cov_grad, scen, scored,
        need, emit, after,
    )
    halving.finish()
    edges.sent()
    out[...] = halving.whole[...]


def run_step(nt, nr, cov, obs, weights):
    seqs, rows, nodes = cov.shape
    w_input, w_filter, w_mixing, w_output = weights
    layers, channels = w_mixing.shape[:2]
    unit = channels // nt
    per = w_output.shape[1] // nodes // nr
    tm_dims, region_dims = bit_dims(nt, nr)
    parts, stages = staged_parts(unit, layers, per, orders_of(tm_dims, region_dims))
    chunk = (per + layers + 1) * unit
    buffers, ends = halving_scratch(tm_dims, region_dims, parts, chunk, nodes)
    vmem, anywhere = pl.BlockSpec(memory_space=pltpu.VMEM), pl.BlockSpec(memory_space=pl.ANY)
    dims = len(tm_dims) + len(region_dims)
    return pl.pallas_call(
        functools.partial(step_kernel, nt, tm_dims, region_dims, parts, stages),
        out_shape=(
            jax.ShapeDtypeStruct(cov.shape, BF16),
            jax.ShapeDtypeStruct((2,) * len(region_dims) + (chunk, nodes), BF16),
        ),
        in_specs=[vmem] * 2 + [anywhere] * 4,
        out_specs=(vmem, vmem),
        scratch_shapes=network_scratch(cov, w_output)
        + [pltpu.VMEM(w.shape, BF16) for w in weights]
        + [
            pltpu.SemaphoreType.DMA((4,)),
            pltpu.VMEM((seqs, 16, nodes), BF16),
            pltpu.VMEM((seqs, 16, nodes), BF16),
            pltpu.VMEM((seqs, HALO, nodes), F32),
            pltpu.VMEM((nt, seqs, 8, 128), F32),
            pltpu.SemaphoreType.DMA((nt + 2,)),
            pltpu.SemaphoreType.DMA((nt + 2,)),
        ]
        + [pltpu.VMEM((2,) * dims + (height, nodes), BF16) for _, height, _ in parts]
        + buffers
        + ends,
        compiler_params=pltpu.CompilerParams(
            collective_id=2, has_side_effects=True, vmem_limit_bytes=56 * 2**20
        ),
        name="step",
    )(cov, obs, *weights)


def unpack_kernel(cov_grad, whole, o_cov, o_input, o_filter, o_mixing, o_output):
    unit, nodes = o_input.shape
    layers = o_filter.shape[0]
    scenarios = o_output.shape[1] // nodes
    per = scenarios // 4

    def piece(sub, at):
        return whole[sub // 2, sub % 2, at * unit : (at + 1) * unit, :]

    o_cov[...] = cov_grad[...]
    for s in range(scenarios):
        o_output[:, s * nodes : (s + 1) * nodes] = piece(s // per, s % per)
    for l in range(layers):
        for h in range(2):
            for q in range(2):
                o_filter[l, q * unit : (q + 1) * unit, h * nodes : (h + 1) * nodes] = piece(
                    h * 2 + q, per + layers - 1 - l
                )
        o_mixing[l] = piece(l, per + layers)
    o_input[...] = piece(layers, per + layers)


def unpack(cov_grad, summed, shapes):
    vmem = pl.BlockSpec(memory_space=pltpu.VMEM)
    shapes = (cov_grad.shape,) + shapes
    return pl.pallas_call(
        unpack_kernel,
        out_shape=tuple(jax.ShapeDtypeStruct(s, BF16) for s in shapes),
        in_specs=[vmem] * 2,
        out_specs=(vmem,) * len(shapes),
        name="unpack",
    )(cov_grad, summed)


def per_device(nt, nr, cov, obs, w_input, w_filter, w_mixing, w_output):
    nodes = cov.shape[2]
    weights = (w_input, w_filter, w_mixing, w_output)
    layers, channels = w_mixing.shape[:2]
    scenarios = w_output.shape[1] // nodes
    unit = channels // nt
    shapes = (
        (unit, nodes), (layers, 2 * unit, 2 * channels), (layers, unit, channels), (unit, scenarios * nodes)
    )
    if unit % 16 == 0 and nr == 4 and layers == 3 and scenarios == 16 and channels == nodes:
        return tuple(unpack(*run_step(nt, nr, cov, obs, weights), shapes))
    edges = exchange_edges(nt, cov, obs)
    cov_grad, *grads = run_network(nt, cov, obs, edges, weights)
    sources = tuple(
        jnp.moveaxis(g.reshape(g.shape[:-2] + (nt, -1) + g.shape[-1:]), -3, 0) for g in grads
    )
    flat = jnp.concatenate([s.reshape(nt, -1) for s in sources], axis=1).reshape(nt, -1, nodes)
    summed = reduce_grads(nt, nr, flat).reshape(-1)
    outs, first = [], 0
    for source, shape in zip(sources, shapes):
        size = source.size // nt
        outs.append(summed[first : first + size].reshape(shape))
        first += size
    return (cov_grad, *outs)


def solution(mesh):
    placed = (P("region", "tm", None), P("region", "tm", None), P(), P(), P(), P())
    return jax.shard_map(
        functools.partial(per_device, mesh.shape["tm"], mesh.shape["region"]),
        mesh=mesh,
        in_specs=placed,
        out_specs=(
            P("region", "tm", None),
            P("tm", None),
            P(None, "tm", None),
            P(None, "tm", None),
            P("tm", None),
        ),
        check_vma=False,
    )
```

```python
import functools

import jax
import jax.numpy as jnp
from jax import lax
from jax.experimental import pallas as pl
from jax.experimental.pallas import tpu as pltpu
from jax.sharding import PartitionSpec as P

MESH = pl.DeviceIdType.MESH
epsilon = 1e-05
HALO = 8
F32 = jnp.float32
BF16 = jnp.bfloat16


def dot(a, b, ca=1, cb=0, precision=None):
    return lax.dot_general(
        a, b, (((ca,), (cb,)), ((), ())), precision=precision, preferred_element_type=F32
    )


class Edges:
    def __init__(self, nt, cov, obs, got_prev, got_next, got_obs, sums, send_sem, recv_sem):
        self.nt, self.cov, self.obs, self.sums = nt, cov, obs, sums
        self.got = (got_prev, got_next, got_obs)
        self.send_sem, self.recv_sem = send_sem, recv_sem
        self.copies = []

    def at(self, offset):
        return {"tm": lax.rem(lax.axis_index("tm") + offset, self.nt)}

    def greet(self, barrier):
        for offset in range(1, self.nt):
            pl.semaphore_signal(barrier, inc=1, device_id=self.at(offset), device_id_type=MESH)

    def own_squares(self):
        seqs, rows, nodes = self.obs.shape
        sq = self.obs[...] * self.obs[...]
        sq = jnp.sum(sq.reshape(seqs, rows // 8, 8, nodes), axis=1)
        own = sq[:, :, :128]
        for part in range(1, nodes // 128):
            own = own + sq[:, :, part * 128 : (part + 1) * 128]
        self.sums[0] = own

    def send(self, src, dst, offset):
        slot = len(self.copies)
        copy = pltpu.make_async_remote_copy(
            src_ref=src, dst_ref=dst,
            send_sem=self.send_sem.at[slot], recv_sem=self.recv_sem.at[slot],
            device_id=self.at(offset), device_id_type=MESH,
        )
        copy.start()
        self.copies.append(copy)

    def start(self):
        nt, rows = self.nt, self.cov.shape[1]
        self.send(self.cov.at[:, pl.ds(rows - 16, 16), :], self.got[0], 1)
        self.send(self.cov.at[:, pl.ds(0, 16), :], self.got[1], nt - 1)
        self.send(self.obs.at[:, pl.ds(0, HALO), :], self.got[2], nt - 1)
        for offset in range(1, nt):
            self.send(self.sums.at[0], self.sums.at[offset], offset)

    def arrived(self, first, last):
        for copy in self.copies[first:last]:
            copy.wait_recv()

    def sent(self):
        for copy in self.copies:
            copy.wait_send()

    def total(self):
        return jnp.sum(self.sums[...], axis=0)


def edges_kernel(nt, cov, obs, prev_cov, next_cov, next_obs, total, *scratch):
    edges = Edges(nt, cov, obs, *scratch)
    barrier = pltpu.get_barrier_semaphore()
    edges.greet(barrier)
    edges.own_squares()
    pl.semaphore_wait(barrier, nt - 1)
    edges.start()
    edges.arrived(0, None)
    edges.sent()
    for out, got in zip((prev_cov, next_cov, next_obs), edges.got):
        out[...] = got[...]
    total[...] = edges.total()


def exchange_edges(nt, cov, obs):
    seqs, rows, nodes = cov.shape
    vmem = pl.BlockSpec(memory_space=pltpu.VMEM)
    edge = jax.ShapeDtypeStruct((seqs, 16, nodes), BF16)
    copies = nt + 2
    return pl.pallas_call(
        functools.partial(edges_kernel, nt),
        out_shape=(
            edge,
            edge,
            jax.ShapeDtypeStruct((seqs, HALO, nodes), F32),
            jax.ShapeDtypeStruct((seqs, 8, 128), F32),
        ),
        in_specs=[vmem] * 2,
        out_specs=(vmem,) * 4,
        scratch_shapes=[
            pltpu.VMEM((seqs, 16, nodes), BF16),
            pltpu.VMEM((seqs, 16, nodes), BF16),
            pltpu.VMEM((seqs, HALO, nodes), F32),
            pltpu.VMEM((nt, seqs, 8, 128), F32),
            pltpu.SemaphoreType.DMA((copies,)),
            pltpu.SemaphoreType.DMA((copies,)),
        ],
        compiler_params=pltpu.CompilerParams(collective_id=0, has_side_effects=True),
        name="edges",
    )(cov, obs)


def network(
    nt, cov, obs, prev_cov, next_cov, next_obs, w_input, w_filter, w_mixing, w_output,
    cov_grad, scen, scored, need, emit, after,
):
    me = lax.axis_index("tm")
    seqs, rows, nodes = cov.shape
    layers = w_filter.shape[0]
    channels = w_mixing.shape[1]
    scenarios = w_output.shape[1] // nodes
    span = rows + 2 * HALO
    kept = rows + HALO
    halves = nodes // 128
    not_first = (me > 0).astype(F32)
    not_last = (me < nt - 1).astype(F32)

    def own_rows(x):
        return jnp.concatenate([x[b * span + HALO : b * span + HALO + rows] for b in range(seqs)], axis=0)

    cov_own = cov[...]
    need("cov")
    need("input")
    spans = []
    for b in range(seqs):
        spans.append(prev_cov[b].astype(F32)[16 - HALO :] * not_first)
        spans.append(cov_own[b].astype(F32))
        spans.append(next_cov[b].astype(F32)[:HALO])
    hidden = dot(jnp.concatenate(spans, axis=0).astype(BF16), w_input[...]).astype(BF16).astype(F32)
    stored = []
    need("filter")
    need("mixing")
    for l in range(layers):
        delayed = pltpu.roll(hidden, 2**l, 0)
        joined = jnp.concatenate([delayed, hidden], axis=1).astype(BF16)
        preact = dot(joined, w_filter[l])
        act = jnp.tanh(preact[:, :channels])
        gate = 0.5 * jnp.tanh(0.5 * preact[:, channels:]) + 0.5
        gated = (act * gate).astype(BF16)
        stored.append((delayed, hidden, act, gate))
        hidden = (hidden + dot(gated, w_mixing[l])).astype(BF16).astype(F32)

    last = jnp.concatenate([hidden[b * span + HALO : (b + 1) * span] for b in range(seqs)], axis=0)
    last = last.astype(BF16)
    need("output")
    batch = 4 if scenarios % 4 == 0 else 1

    def columns(s):
        return pl.ds(pl.multiple_of(s * nodes, nodes), nodes)

    def predict(j, carry):
        for k in range(batch):
            s = j * batch + k
            pred = dot(last, w_output[:, columns(s)])
            for h in range(halves):
                scen[h, pl.ds(s, seqs * kept, stride=scenarios), :] = pred[:, h * 128 : (h + 1) * 128]
        return carry

    lax.fori_loop(0, scenarios // batch, predict, 0)
    need("obs")
    for b in range(seqs):
        scored[b * kept : b * kept + rows] = obs[b]
        scored[b * kept + rows : (b + 1) * kept] = next_obs[b]

    block = 16 * scenarios
    row_no = lax.broadcasted_iota(jnp.int32, (block, block), 0)
    col_no = lax.broadcasted_iota(jnp.int32, (block, block), 1)
    same_step = (row_no // scenarios) == (col_no // scenarios)
    diagonal = row_no == col_no
    pairs = jnp.where(same_step & ~diagonal, 1.0 / (scenarios * (scenarios - 1) * nodes), 0.0)

    def score(groups):
        ats = [pl.ds(pl.multiple_of(g * block, block), block) for g in groups]
        ys = [jnp.concatenate([scen[h, at, :] for h in range(halves)], axis=1) for at in ats]
        highs = [y.astype(BF16) for y in ys]
        lows = [(y - hi.astype(F32)).astype(BF16) for y, hi in zip(ys, highs)]
        grams = [
            dot(jnp.concatenate([hi, lo, hi, lo], axis=1), jnp.concatenate([hi, hi, lo, lo], axis=1), 1, 1)
            for hi, lo in zip(highs, lows)
        ]
        targets = []
        for g, y in zip(groups, ys):
            o = scored[pl.ds(pl.multiple_of(g * 16, 16), 16), :]
            diff = y - jnp.broadcast_to(o[:, None, :], (16, scenarios, nodes)).reshape(block, nodes)
            inv = lax.rsqrt(jnp.sum(diff * diff, axis=1, keepdims=True) * (1.0 / nodes) + epsilon)
            targets.append(inv * (1.0 / (scenarios * nodes)) * diff)
        coefs = []
        for gram in grams:
            own = jnp.where(diagonal, gram, 0.0)
            own_sq = jnp.sum(own, axis=1, keepdims=True) + jnp.sum(own, axis=0, keepdims=True)
            pair_sq = jnp.maximum(own_sq - 2.0 * gram, 0.0) * (1.0 / nodes)
            coefs.append(pairs * lax.rsqrt(pair_sq + epsilon))
        for at, y, hi, lo, coef, target in zip(ats, ys, highs, lows, coefs, targets):
            chi = coef.astype(BF16)
            clo = (coef - chi.astype(F32)).astype(BF16)
            mixed = dot(jnp.concatenate([chi, clo, chi], axis=1), jnp.concatenate([hi, hi, lo], axis=0))
            grad = mixed - jnp.sum(coef, axis=1, keepdims=True) * y + target
            for h in range(halves):
                scen[h, at, :] = grad[:, h * 128 : (h + 1) * 128]

    groups = seqs * kept // 16

    def score_pair(i, carry):
        score([2 * i, 2 * i + 1])
        return carry

    lax.fori_loop(0, groups // 2, score_pair, 0)
    if groups % 2:
        score([groups - 1])

    length = rows * nt
    step_no = lax.broadcasted_iota(jnp.int32, (kept, 1), 0)
    valid = jnp.where(step_no < rows, 1.0, not_last)
    factor = []
    total = need("total")
    for b in range(seqs):
        sq = jnp.sum(jnp.sum(total[b], axis=1, keepdims=True), axis=0, keepdims=True)
        factor.append(valid * lax.rsqrt(sq / (length * nodes) + epsilon))
    factor = jnp.concatenate(factor, axis=0)

    def kept_own(x):
        return jnp.concatenate([x[b * kept : b * kept + rows] for b in range(seqs)], axis=0)

    last_own = own_rows(hidden).T.astype(BF16)

    def output_step(j, grad_last):
        for k in range(batch):
            s = j * batch + k
            g = jnp.concatenate(
                [scen[h, pl.ds(s, seqs * kept, stride=scenarios), :] for h in range(halves)], axis=1
            )
            g = g * factor
            grad_last = grad_last + dot(g.astype(BF16), w_output[:, columns(s)], 1, 1)
            emit("output", (j, k), dot(last_own, kept_own(g).astype(BF16)))
        return grad_last

    grad_last = jnp.zeros((seqs * kept, channels), F32)
    grad_last = lax.fori_loop(0, scenarios // batch, output_step, grad_last)
    after("output")
    grad_last = grad_last.astype(BF16).astype(F32)
    pieces = []
    for b in range(seqs):
        pieces.append(jnp.zeros((HALO, channels), F32))
        pieces.append(grad_last[b * kept : (b + 1) * kept])
    grad = jnp.concatenate(pieces, axis=0)

    for l in reversed(range(layers)):
        delayed, held, act, gate = stored[l]
        grad16 = grad.astype(BF16)
        gated_t = own_rows(act * gate).T.astype(BF16)
        part = dot(gated_t, own_rows(grad).astype(BF16))
        emit("mixing", l, part)
        gated_cot = dot(grad16, w_mixing[l], 1, 1).astype(BF16).astype(F32)
        pre = jnp.concatenate(
            [gated_cot * gate * (1.0 - act * act), gated_cot * act * gate * (1.0 - gate)], axis=1
        )
        own_pre = own_rows(pre).astype(BF16)
        for tap, source in enumerate((delayed, held)):
            part = dot(own_rows(source).T.astype(BF16), own_pre)
            emit("filter", (l, tap), part)
        after(l)
        both = dot(pre.astype(BF16), w_filter[l], 1, 1).astype(BF16).astype(F32)
        past = pltpu.roll(both[:, :channels], seqs * span - 2**l, 0)
        grad = (grad + both[:, channels:] + past).astype(BF16).astype(F32)

    own = own_rows(grad).astype(BF16)
    cov_flat = jnp.concatenate([cov_own[b] for b in range(seqs)], axis=0)
    part = dot(cov_flat.astype(F32).T.astype(BF16), own)
    emit("input", None, part)
    after("input")
    result = dot(own, w_input[...], 1, 1).astype(BF16)
    for b in range(seqs):
        cov_grad[b] = result[b * rows : (b + 1) * rows]


def network_kernel(nt, cov, obs, prev_cov, next_cov, next_obs, total, *rest):
    weights, cov_grad, grads, (scen, scored) = rest[:4], rest[4], rest[5:9], rest[9:]
    g_input, g_filter, g_mixing, g_output = grads
    nodes, channels = cov.shape[2], weights[2].shape[1]

    def need(name):
        return total[...] if name == "total" else None

    def emit(name, index, part):
        part = part.astype(BF16)
        if name == "output":
            j, k = index
            batch = 4 if g_output.shape[1] // nodes % 4 == 0 else 1
            g_output[:, pl.ds(pl.multiple_of((j * batch + k) * nodes, nodes), nodes)] = part
        elif name == "mixing":
            g_mixing[index] = part
        elif name == "filter":
            l, tap = index
            g_filter[l, tap * channels : (tap + 1) * channels, :] = part
        else:
            g_input[...] = part

    network(
        nt, cov, obs, prev_cov, next_cov, next_obs, *weights, cov_grad, scen, scored,
        need, emit, lambda stage: None,
    )


def network_scratch(cov, w_output):
    seqs, rows, nodes = cov.shape
    steps = seqs * (rows + HALO)
    scenarios = w_output.shape[1] // nodes
    return [
        pltpu.VMEM((nodes // 128, steps * scenarios, 128), F32),
        pltpu.VMEM((steps, nodes), F32),
    ]


def run_network(nt, cov, obs, edges, weights):
    vmem = pl.BlockSpec(memory_space=pltpu.VMEM)
    grads = tuple(jax.ShapeDtypeStruct(w.shape, BF16) for w in weights)
    return pl.pallas_call(
        functools.partial(network_kernel, nt),
        out_shape=(jax.ShapeDtypeStruct(cov.shape, BF16),) + grads,
        in_specs=[vmem] * 10,
        out_specs=(vmem,) * (1 + len(grads)),
        scratch_shapes=network_scratch(cov, weights[3]),
        compiler_params=pltpu.CompilerParams(vmem_limit_bytes=56 * 2**20),
        name="network",
    )(cov, obs, *edges, *weights)


def bit_dims(nt, nr):
    bits = lambda n: n.bit_length() - 1
    tm_dims = [("tm", 2**i) for i in reversed(range(bits(nt)))]
    region_dims = [("region", 2**i) for i in reversed(range(bits(nr)))]
    return tm_dims, region_dims


def orders_of(tm_dims, region_dims):
    near = region_dims[-1:]
    x, ys = region_dims[:-1], list(reversed(tm_dims))
    y, z = ys[:1], ys[1:]
    return [near + x + y + z, near + y + z[:1] + x + z[1:], near + z[:1] + x + y + z[1:]]


def even_parts(rows, orders):
    units = rows // 16
    count = min(2 * len(orders), units)
    cuts = [16 * (units * i // count) for i in range(count + 1)]
    return [(cuts[i], cuts[i + 1] - cuts[i], orders[i % 3]) for i in range(count)]


class Halving:
    def __init__(self, sources, tm_dims, region_dims, parts, buffers, whole, send_sem, recv_sem):
        self.dims, self.region_dims, self.parts = tm_dims + region_dims, region_dims, parts
        self.whole = whole
        self.send_sem, self.recv_sem = send_sem, recv_sem
        n = len(self.dims)
        self.buffers = [buffers[i * n : (i + 1) * n] for i in range(len(parts))]
        self.current = list(sources)
        self.phase = [0 for _ in parts]
        self.flying = [None for _ in parts]
        self.done = []
        self.slot = 0
        self.where = {"tm": lax.axis_index("tm"), "region": lax.axis_index("region")}

    def bit(self, dim):
        axis, weight = dim
        return lax.rem(lax.div(self.where[axis], weight), 2)

    def across(self, dim):
        axis, weight = dim
        return {axis: self.where[axis] + weight * (1 - 2 * self.bit(dim))}

    def copy(self, i, src, dst, dim):
        copy = pltpu.make_async_remote_copy(
            src_ref=src, dst_ref=dst,
            send_sem=self.send_sem.at[self.slot], recv_sem=self.recv_sem.at[self.slot],
            device_id=self.across(dim), device_id_type=MESH,
        )
        self.slot += 1
        copy.start()
        self.flying[i] = copy

    def rows_at(self, i):
        return pl.ds(self.parts[i][0], self.parts[i][1])

    def send_half(self, i):
        dim = self.parts[i][2][self.phase[i]]
        self.copy(i, self.current[i].at[1 - self.bit(dim)], self.buffers[i][self.phase[i]], dim)

    def send_whole(self, i, n):
        index = tuple(slice(None) if m < n else self.bit(d) for m, d in enumerate(self.region_dims))
        index = index + (self.rows_at(i), slice(None))
        self.copy(i, self.whole.at[index], self.whole.at[index], self.region_dims[n])

    def begin(self, i):
        self.send_half(i)

    def advance(self, i):
        if self.flying[i] is None:
            return False
        self.flying[i].wait_recv()
        self.done.append(self.flying[i])
        self.flying[i] = None
        phase, last = self.phase[i], len(self.dims)
        if phase < last:
            dim = self.parts[i][2][phase]
            into = self.buffers[i][phase]
            mine = self.current[i][self.bit(dim)]
            into[...] = (into[...].astype(F32) + mine.astype(F32)).astype(BF16)
            self.current[i] = into
            self.phase[i] += 1
            if phase + 1 < last:
                self.send_half(i)
            else:
                index = tuple(self.bit(d) for d in self.region_dims)
                self.whole[index + (self.rows_at(i), slice(None))] = into[...]
                self.send_whole(i, 0)
        else:
            self.phase[i] += 1
            if phase + 1 - last < len(self.region_dims):
                self.send_whole(i, phase + 1 - last)
        return True

    def round(self):
        return any([self.advance(i) for i in range(len(self.parts))])

    def finish(self):
        while self.round():
            pass
        for copy in self.done:
            copy.wait_send()


def halving_scratch(tm_dims, region_dims, parts, rows, nodes):
    n = len(tm_dims) + len(region_dims)
    scratch = []
    for _, height, _ in parts:
        for phase in range(n):
            scratch.append(pltpu.VMEM((2,) * (n - phase - 1) + (height, nodes), BF16))
    copies = len(parts) * (n + len(region_dims))
    return scratch, [
        pltpu.VMEM((2,) * len(region_dims) + (rows, nodes), BF16),
        pltpu.SemaphoreType.DMA((copies,)),
        pltpu.SemaphoreType.DMA((copies,)),
    ]


def reduce_kernel(tm_dims, region_dims, parts, *refs):
    sources, out, refs = refs[: len(parts)], refs[len(parts)], refs[len(parts) + 1 :]
    halving = Halving(sources, tm_dims, region_dims, parts, refs[:-3], *refs[-3:])
    barrier = pltpu.get_barrier_semaphore()
    for dim in halving.dims:
        pl.semaphore_signal(barrier, inc=1, device_id=halving.across(dim), device_id_type=MESH)
    pl.semaphore_wait(barrier, len(halving.dims))
    for i in range(len(parts)):
        halving.begin(i)
    halving.finish()
    out[...] = halving.whole[...]


def reduce_grads(nt, nr, grads):
    _, width, nodes = grads.shape
    rows = width // nr
    tm_dims, region_dims = bit_dims(nt, nr)
    parts = even_parts(rows, orders_of(tm_dims, region_dims))
    grads = grads.reshape((2,) * (len(tm_dims) + len(region_dims)) + (rows, nodes))
    dims = tm_dims + region_dims
    sources = []
    for start, height, order in parts:
        moved = tuple(dims.index(d) for d in order) + (len(dims), len(dims) + 1)
        sources.append(jnp.transpose(grads[..., start : start + height, :], moved))
    buffers, ends = halving_scratch(tm_dims, region_dims, parts, rows, nodes)
    vmem = pl.BlockSpec(memory_space=pltpu.VMEM)
    return pl.pallas_call(
        functools.partial(reduce_kernel, tm_dims, region_dims, parts),
        out_shape=jax.ShapeDtypeStruct((2,) * len(region_dims) + (rows, nodes), BF16),
        in_specs=[vmem] * len(sources),
        out_specs=vmem,
        scratch_shapes=buffers + ends,
        compiler_params=pltpu.CompilerParams(
            collective_id=1, has_side_effects=True, vmem_limit_bytes=56 * 2**20
        ),
        name="reduce",
    )(*sources)


def staged_parts(unit, layers, per, orders):
    by_x, by_y, by_z = orders
    third = per * unit // 3 // 16 * 16
    early = per * unit - 2 * third
    parts, stages = [], {}

    def add(stage, start, height, order):
        stages.setdefault(stage, []).append(len(parts))
        parts.append((start, height, order))

    add("output", 0, early - (early - third) // 2 // 16 * 16, by_x)
    second = parts[0][1]
    add("output", second, per * unit - second - third, by_y)
    add("output", per * unit - third, third, by_z)
    early_layers = (layers + 1) // 2
    add(layers - early_layers, per * unit, early_layers * unit, by_z)
    tail = (per + early_layers) * unit
    rest = (layers + 1 - early_layers) * unit
    cut = rest // 2 // 16 * 16
    add("input", tail, cut, by_x)
    add("input", tail + cut, rest - cut, by_y)
    return parts, stages


def step_kernel(
    nt, tm_dims, region_dims, parts, stages,
    cov, obs, w_input, w_filter, w_mixing, w_output, cov_grad, out,
    scen, scored, v_input, v_filter, v_mixing, v_output, load_sem, *refs,
):
    edges = Edges(nt, cov, obs, *refs[:6])
    sources, refs = refs[6 : 6 + len(parts)], refs[len(parts) :]
    halving = Halving(sources, tm_dims, region_dims, parts, refs[6:-3], *refs[-3:])
    barrier = pltpu.get_barrier_semaphore()
    edges.greet(barrier)
    for dim in region_dims:
        pl.semaphore_signal(barrier, inc=1, device_id=halving.across(dim), device_id_type=MESH)
    loads = {}
    pairs = (("input", w_input, v_input), ("filter", w_filter, v_filter),
             ("mixing", w_mixing, v_mixing), ("output", w_output, v_output))
    for n, (name, src, dst) in enumerate(pairs):
        loads[name] = pltpu.make_async_copy(src, dst, load_sem.at[n])
        loads[name].start()
    edges.own_squares()
    pl.semaphore_wait(barrier, nt - 1 + len(region_dims))
    edges.start()

    nodes = cov.shape[2]
    layers, channels = w_mixing.shape[:2]
    unit = channels // nt
    per = w_output.shape[1] // nodes // 4
    every = range(nt)

    def need(name):
        if name == "cov":
            edges.arrived(0, 2)
        elif name == "obs":
            edges.arrived(2, 3)
        elif name == "total":
            edges.arrived(3, None)
            return edges.total()
        else:
            loads[name].wait()

    def put(owners, sub, at, value):
        value = value.reshape(len(owners), unit, nodes).astype(BF16)
        place = {("region", 2): lax.div(sub, 2), ("region", 1): lax.rem(sub, 2)}
        for source, (start, height, order) in zip(sources, parts):
            low, high = max(start, at * unit), min(start + height, (at + 1) * unit)
            if low >= high:
                continue
            for j, owner in enumerate(owners):
                index = tuple(place[d] if d in place else owner // d[1] % 2 for d in order)
                index = index + (slice(low - start, high - start), slice(None))
                source[index] = value[j, low - at * unit : high - at * unit]

    def emit(name, index, part):
        if name == "output":
            put(every, index[0], index[1], part)
        elif name == "mixing":
            put(every, index, per + layers, part)
        elif name == "input":
            put(every, layers, per + layers, part)
        else:
            l, tap = index
            owners = range(tap * nt // 2, (tap + 1) * nt // 2)
            for h in range(2):
                piece = part[:, h * nodes : (h + 1) * nodes].reshape(nt // 2, 2, unit, nodes)
                for q in range(2):
                    put(owners, h * 2 + q, per + layers - 1 - l, piece[:, q])

    def after(stage):
        if stage == 0:
            for i in stages["output"]:
                halving.advance(i)
        for i in stages.get(stage, []):
            halving.begin(i)

    network(
        nt, cov, obs, *edges.got, v_input, v_filter, v_mixing, v_output, cov_grad, scen, scored,
        need, emit, after,
    )
    halving.finish()
    edges.sent()
    out[...] = halving.whole[...]


def run_step(nt, nr, cov, obs, weights):
    seqs, rows, nodes = cov.shape
    w_input, w_filter, w_mixing, w_output = weights
    layers, channels = w_mixing.shape[:2]
    unit = channels // nt
    per = w_output.shape[1] // nodes // nr
    tm_dims, region_dims = bit_dims(nt, nr)
    parts, stages = staged_parts(unit, layers, per, orders_of(tm_dims, region_dims))
    chunk = (per + layers + 1) * unit
    buffers, ends = halving_scratch(tm_dims, region_dims, parts, chunk, nodes)
    vmem, anywhere = pl.BlockSpec(memory_space=pltpu.VMEM), pl.BlockSpec(memory_space=pl.ANY)
    dims = len(tm_dims) + len(region_dims)
    return pl.pallas_call(
        functools.partial(step_kernel, nt, tm_dims, region_dims, parts, stages),
        out_shape=(
            jax.ShapeDtypeStruct(cov.shape, BF16),
            jax.ShapeDtypeStruct((2,) * len(region_dims) + (chunk, nodes), BF16),
        ),
        in_specs=[vmem] * 2 + [anywhere] * 4,
        out_specs=(vmem, vmem),
        scratch_shapes=network_scratch(cov, w_output)
        + [pltpu.VMEM(w.shape, BF16) for w in weights]
        + [
            pltpu.SemaphoreType.DMA((4,)),
            pltpu.VMEM((seqs, 16, nodes), BF16),
            pltpu.VMEM((seqs, 16, nodes), BF16),
            pltpu.VMEM((seqs, HALO, nodes), F32),
            pltpu.VMEM((nt, seqs, 8, 128), F32),
            pltpu.SemaphoreType.DMA((nt + 2,)),
            pltpu.SemaphoreType.DMA((nt + 2,)),
        ]
        + [pltpu.VMEM((2,) * dims + (height, nodes), BF16) for _, height, _ in parts]
        + buffers
        + ends,
        compiler_params=pltpu.CompilerParams(
            collective_id=2, has_side_effects=True, vmem_limit_bytes=56 * 2**20
        ),
        name="step",
    )(cov, obs, *weights)


def unpack_kernel(cov_grad, whole, o_cov, o_input, o_filter, o_mixing, o_output):
    unit, nodes = o_input.shape
    layers = o_filter.shape[0]
    scenarios = o_output.shape[1] // nodes
    per = scenarios // 4

    def piece(sub, at):
        return whole[sub // 2, sub % 2, at * unit : (at + 1) * unit, :]

    o_cov[...] = cov_grad[...]
    for s in range(scenarios):
        o_output[:, s * nodes : (s + 1) * nodes] = piece(s // per, s % per)
    for l in range(layers):
        for h in range(2):
            for q in range(2):
                o_filter[l, q * unit : (q + 1) * unit, h * nodes : (h + 1) * nodes] = piece(
                    h * 2 + q, per + layers - 1 - l
                )
        o_mixing[l] = piece(l, per + layers)
    o_input[...] = piece(layers, per + layers)


def unpack(cov_grad, summed, shapes):
    vmem = pl.BlockSpec(memory_space=pltpu.VMEM)
    shapes = (cov_grad.shape,) + shapes
    return pl.pallas_call(
        unpack_kernel,
        out_shape=tuple(jax.ShapeDtypeStruct(s, BF16) for s in shapes),
        in_specs=[vmem] * 2,
        out_specs=(vmem,) * len(shapes),
        name="unpack",
    )(cov_grad, summed)


def per_device(nt, nr, cov, obs, w_input, w_filter, w_mixing, w_output):
    nodes = cov.shape[2]
    weights = (w_input, w_filter, w_mixing, w_output)
    layers, channels = w_mixing.shape[:2]
    scenarios = w_output.shape[1] // nodes
    unit = channels // nt
    shapes = (
        (unit, nodes), (layers, 2 * unit, 2 * channels), (layers, unit, channels), (unit, scenarios * nodes)
    )
    if unit % 16 == 0 and nr == 4 and layers == 3 and scenarios == 16 and channels == nodes:
        return tuple(unpack(*run_step(nt, nr, cov, obs, weights), shapes))
    edges = exchange_edges(nt, cov, obs)
    cov_grad, *grads = run_network(nt, cov, obs, edges, weights)
    sources = tuple(
        jnp.moveaxis(g.reshape(g.shape[:-2] + (nt, -1) + g.shape[-1:]), -3, 0) for g in grads
    )
    flat = jnp.concatenate([s.reshape(nt, -1) for s in sources], axis=1).reshape(nt, -1, nodes)
    summed = reduce_grads(nt, nr, flat).reshape(-1)
    outs, first = [], 0
    for source, shape in zip(sources, shapes):
        size = source.size // nt
        outs.append(summed[first : first + size].reshape(shape))
        first += size
    return (cov_grad, *outs)


def solution(mesh):
    placed = (P("region", "tm", None), P("region", "tm", None), P(), P(), P(), P())
    return jax.shard_map(
        functools.partial(per_device, mesh.shape["tm"], mesh.shape["region"]),
        mesh=mesh,
        in_specs=placed,
        out_specs=(
            P("region", "tm", None),
            P("tm", None),
            P(None, "tm", None),
            P(None, "tm", None),
            P("tm", None),
        ),
        check_vma=False,
    )
```
